256 devices in a mesh: fsdp: 64 (over y_lo, z, x), dp: 4 (over y_hi, core).
Axes of the slice: x: 4, y: 4 (y_hi: 2, y_lo: 2; y = y_hi * 2 + y_lo), z: 8, core: 2. Of those that a mesh axis runs over, the one named last changes fastest.
Arguments:
- tokens: bfloat16 [32768, 2048], P(('dp', 'fsdp')), may hold values from -6 to 6
- cotangent: bfloat16 [32768, 8192], P('dp', 'fsdp'), may hold values from -125 to 125
- weight: float32 [2048, 8192], P(None, 'fsdp'), may hold values from -0.125 to 0.125
- probe_bits: int32 [2048, 8192], P(None, 'fsdp'), may hold values from 0 to 1
- moment: float32 [2048, 8192], P(None, 'fsdp'), may hold values from -3 to 3
- curvature: float32 [2048, 8192], P(None, 'fsdp'), may hold values from 0.2 to 2
Outputs:
- moment_out: float32 [2048, 8192], P(None, 'fsdp')
- curvature_out: float32 [2048, 8192], P(None, 'fsdp')
- update: float32 [2048, 8192], P(None, 'fsdp')
The draws below stay inside these ranges and needn't reach their ends.
All inputs are finite; a program needn't handle non-finite values.
Results may differ from the reference program's by a relative error of at most 0.0055.
Values may be sent and summed in bfloat16 or wider, within the bound.
No kernel may reach another device: no remote copies, remote signals or barrier semaphores. Data moves between devices by JAX's collectives and lax.ppermute only.
A program may use at most 128 MiB of HBM per device.

```python
import math
import jax
import jax.numpy as jnp
from jax import lax

D = 2048
FF = 8192
TOK_DEV = 128
HESS_DEV = 64
TOKENS = 32768


def draw_cotangent(key, part):
    key = jax.random.fold_in(key, 11)
    key_base, key_rows, key_cols = jax.random.split(key, 3)
    row_scale = jnp.exp(jax.random.uniform(key_rows, (TOKENS, 1), jnp.float32) * jnp.log(10.0))
    rising = jnp.exp(jnp.log(3.0) * jnp.arange(FF, dtype=jnp.float32) / FF)
    col_scale = jnp.exp(jax.random.uniform(key_cols, (1, FF), jnp.float32) * jnp.log(10.0)) * rising[None, :]
    base = jnp.clip(jax.random.normal(key_base, (TOKENS, FF), jnp.float32), -4.0, 4.0)
    return (0.1 * base * row_scale * col_scale).astype(jnp.bfloat16)


def set_ends(drawn, rng, smallest, largest):
    place = [jax.random.randint(jax.random.fold_in(rng, axis), (), 0, length) for axis, length in enumerate(drawn.shape)]
    widest = drawn.shape.index(max(drawn.shape))
    next_to = place[:widest] + [(place[widest] + 1) % drawn.shape[widest]] + place[widest + 1:]
    return drawn.at[tuple(place)].set(smallest).at[tuple(next_to)].set(largest)


def shard_levels(key, shape, shards, least, largest):
    def one(position, blocks):
        draws = jax.random.uniform(jax.random.fold_in(jax.random.fold_in(key, 6), position), (blocks,), jnp.float32, least / len(shards), largest / len(shards))
        return jnp.repeat(jnp.exp(draws), shape[position] // blocks).reshape((-1,) + (1,) * (len(shape) - position - 1))

    factor_of = one(*shards[0])
    for cut in shards[1:]:
        factor_of = factor_of * one(*cut)
    return factor_of


def normal_values(key, dims, deviation, limit, shards=(), held_as=jnp.bfloat16):
    gain = shard_levels(key, dims, shards, -0.22, 0.18) if shards else 1.0
    entries = jax.random.normal(key, dims, jnp.float32) * deviation * gain
    return jnp.minimum(jnp.maximum(entries, -limit), limit).astype(held_as)


def setup_inputs(seed: int = 0) -> dict:
    key_of = jax.random.split(jax.random.key(seed), 7)
    tokens = normal_values(key_of[0], (TOKENS, D), 1.0, 6.0, ((0, 256),))
    cotangent = draw_cotangent(jax.random.fold_in(key_of[6], 71), 0)
    weight = normal_values(key_of[2], (D, FF), D ** -0.5, 0.125, ((1, 64),), jnp.float32)
    probe_bits = set_ends(jax.random.randint(key_of[3], (D, FF), 0, 2), jax.random.fold_in(key_of[3], 1), 0, 1).astype(jnp.int32)
    moment = normal_values(key_of[4], (D, FF), 0.5, 3.0, ((1, 64),), jnp.float32)
    curvature = jnp.clip(0.2 + 1.8 * jax.random.uniform(key_of[5], (D, FF), jnp.float32) ** shard_levels(key_of[5], (D, FF), ((1, 64),), -0.2, 0.2), 0.2, 2.0)
    return {"tokens": tokens, "cotangent": cotangent, "weight": weight, "probe_bits": probe_bits, "moment": moment, "curvature": curvature}


inv_root_two = 0.7071067811865476
inv_root_tau = 0.3989422804014327
beta_first = 0.96
beta_second = 0.99
gamma_scale = 0.5
floor_value = 0.1

def gelu_slopes(values):
    density = jnp.exp(-0.5 * values * values) * inv_root_tau
    normal_cdf = 0.5 * (1.0 + lax.erf(values * inv_root_two))
    return (normal_cdf + values * density, density * (2.0 - values * values))

def reference(tokens, cotangent, weight, probe_bits, moment, curvature):
    wbf = weight.astype(jnp.bfloat16)
    probe = (2 * probe_bits - 1).astype(jnp.bfloat16)
    blocks_dev = TOKENS // TOK_DEV
    hess_tokens = tokens.reshape(blocks_dev, TOK_DEV, D)[:, :HESS_DEV].reshape(blocks_dev * HESS_DEV, D)
    hess_cot = cotangent.reshape(blocks_dev, TOK_DEV, FF)[:, :HESS_DEV].reshape(blocks_dev * HESS_DEV, FF)
    width_block = math.gcd(FF, 512)
    count_blocks = FF // width_block

    def one_block(number):
        start = (number * width_block).astype(jnp.int32)
        w_block = lax.dynamic_slice_in_dim(wbf, start, width_block, 1)
        p_block = lax.dynamic_slice_in_dim(probe, start, width_block, 1)
        c_block = lax.dynamic_slice_in_dim(cotangent, start, width_block, 1)
        ch_block = lax.dynamic_slice_in_dim(hess_cot, start, width_block, 1)
        pre = jnp.dot(tokens, w_block, preferred_element_type=jnp.float32)
        slope, unused = gelu_slopes(pre)
        first = (c_block.astype(jnp.float32) * slope).astype(jnp.bfloat16)
        pre_hess = jnp.dot(hess_tokens, w_block, preferred_element_type=jnp.float32)
        tangent = jnp.dot(hess_tokens, p_block, preferred_element_type=jnp.float32)
        unused_two, bend = gelu_slopes(pre_hess)
        second = (ch_block.astype(jnp.float32) * bend * tangent).astype(jnp.bfloat16)
        grad_block = lax.dot_general(tokens, first, (((0,), (0,)), ((), ())), preferred_element_type=jnp.float32)
        hess_block = lax.dot_general(hess_tokens, second, (((0,), (0,)), ((), ())), preferred_element_type=jnp.float32)
        return (grad_block, hess_block)
    grads, hessians = lax.map(one_block, jnp.arange(count_blocks, dtype=jnp.int32))
    gradient = jnp.transpose(grads, (1, 0, 2)).reshape(D, FF)
    hessian_vector = jnp.transpose(hessians, (1, 0, 2)).reshape(D, FF)
    squares = jnp.sum(gradient * gradient)
    scale = jnp.minimum(1.0, lax.rsqrt(squares / (D * FF) + 1e-06))
    estimate = 2.0 * scale * probe.astype(jnp.float32) * hessian_vector
    moment_out = beta_first * moment + (1.0 - beta_first) * scale * gradient
    curvature_out = beta_second * curvature + (1.0 - beta_second) * estimate
    update = jnp.clip(moment_out / jnp.maximum(gamma_scale * curvature_out, floor_value), -1.0, 1.0)
    return (moment_out, curvature_out, update)
```

```python
import jax
import jax.numpy as jnp
from jax import lax
from jax.sharding import Mesh, PartitionSpec as P

D = 2048
FF = 8192


inv_root_two = 0.7071067811865476
inv_root_tau = 0.3989422804014327
beta_first = 0.96
beta_second = 0.99
gamma_scale = 0.5
floor_value = 0.1

SIZES = {"yl": 2, "z": 8, "x": 4, "yh": 2, "c": 2}
AXES = tuple(SIZES)


def gelu_slopes(values):
    density = jnp.exp(-0.5 * values * values) * inv_root_tau
    normal_cdf = 0.5 * (1.0 + lax.erf(values * inv_root_two))
    return (normal_cdf + values * density, density * (2.0 - values * values))


def transposed(left, right):
    return lax.dot_general(
        left, right, (((0,), (0,)), ((), ())), preferred_element_type=jnp.float32
    )


def sophia_step(gradient, hessian_vector, probe, moment, curvature, squares):
    scale = jnp.minimum(1.0, lax.rsqrt(squares / (D * FF) + 1e-06))
    estimate = 2.0 * scale * probe.astype(jnp.float32) * hessian_vector
    moment_out = beta_first * moment + (1.0 - beta_first) * scale * gradient
    curvature_out = beta_second * curvature + (1.0 - beta_second) * estimate
    update = jnp.clip(moment_out / jnp.maximum(gamma_scale * curvature_out, floor_value), -1.0, 1.0)
    return (moment_out, curvature_out, update)


def shift(value, axis, by):
    n = SIZES[axis]
    return lax.ppermute(value, axis, [(i, (i + by) % n) for i in range(n)])


def gather_tokens(tokens):
    got = {(0, 0): tokens}
    got[0, -1] = shift(tokens, "z", 1)
    got[0, 1] = shift(tokens, "z", -1)
    got[1, 0] = shift(tokens, "yl", 1)
    got[0, -2] = shift(got[0, -1], "z", 1)
    got[0, 2] = shift(got[0, 1], "z", -1)
    got[1, -1] = shift(got[0, -1], "yl", 1)
    got[0, -3] = shift(got[0, -2], "z", 1)
    got[0, 3] = shift(got[0, 2], "z", -1)
    got[1, -2] = shift(got[0, -2], "yl", 1)
    got[0, -4] = shift(got[0, -3], "z", 1)
    got[1, 1] = shift(got[1, 0], "z", -1)
    got[1, -3] = shift(got[0, -3], "yl", 1)
    got[1, -4] = shift(got[1, -3], "z", 1)
    got[1, 2] = shift(got[1, 1], "z", -1)
    got[1, 3] = shift(got[0, 3], "yl", 1)
    return got


GROUPS = (
    ((0, 0), (0, -1), (0, 1), (1, 0)),
    ((0, -2), (0, 2), (1, -1), (0, -3), (0, 3), (1, -2)),
    ((0, -4), (1, 1), (1, -3), (1, -4), (1, 2), (1, 3)),
)
HOPS = (0, 1, -1, 2)


def local(tokens, cotangent, weight, probe_bits, moment, curvature):
    tok_dev, width = tokens.shape
    hess_dev = tok_dev // 2
    hidden = weight.shape[1]
    place = {axis: lax.axis_index(axis) for axis in AXES}
    wbf = weight.astype(jnp.bfloat16)
    probe = (2 * probe_bits - 1).astype(jnp.bfloat16)

    mine = jnp.where(place["c"] == 0, wbf, probe)
    mine = [mine] + [shift(mine, "x", hop) for hop in HOPS[1:]]
    mine = jnp.concatenate(mine, axis=1)
    theirs = shift(mine, "c", 1)
    weights = jnp.where(place["c"] == 0, mine, theirs)
    probes = jnp.where(place["c"] == 0, theirs, mine)

    blocks = cotangent.reshape(2, 8, 4, tok_dev, hidden)
    parts = []
    for hop in HOPS:
        part = lax.dynamic_index_in_dim(blocks, (place["x"] + hop) % 4, 2, keepdims=False)
        parts.append(part if hop == 0 else shift(part, "x", hop))
    upstream = jnp.concatenate(parts, axis=-1)
    upstream = jnp.concatenate((upstream, upstream), axis=1)
    upstream = lax.dynamic_slice_in_dim(upstream, place["z"], 8, 1)
    upstream = jnp.where(place["yl"] == 0, upstream, upstream[::-1])

    got = gather_tokens(tokens)

    gradient = hessian_vector = 0.0
    for group in GROUPS:
        piece_hess = jnp.concatenate([got[key][:hess_dev] for key in group])
        piece = jnp.concatenate([piece_hess] + [got[key][hess_dev:] for key in group])
        up = jnp.concatenate(
            [upstream[s, dz % 8, :hess_dev] for s, dz in group]
            + [upstream[s, dz % 8, hess_dev:] for s, dz in group]
        ).astype(jnp.float32)
        rows = piece_hess.shape[0]
        pre = jnp.dot(piece, weights, preferred_element_type=jnp.float32)
        tangent = jnp.dot(piece_hess, probes, preferred_element_type=jnp.float32)
        slope, bend = gelu_slopes(pre)
        first = (up * slope).astype(jnp.bfloat16)
        second = (up[:rows] * bend[:rows] * tangent).astype(jnp.bfloat16)
        gradient = gradient + transposed(piece, first)
        hessian_vector = hessian_vector + transposed(piece_hess, second)

    half = width // 2

    def reduced(partial):
        keep = lax.dynamic_slice_in_dim(partial, place["c"] * half, half, 0)
        give = lax.dynamic_slice_in_dim(partial, (1 - place["c"]) * half, half, 0)
        keep = keep + shift(give.astype(jnp.bfloat16), "c", 1).astype(jnp.float32)
        total = keep[:, :hidden]
        for number, hop in enumerate(HOPS):
            if number:
                sent = keep[:, number * hidden : (number + 1) * hidden].astype(jnp.bfloat16)
                total = total + shift(sent, "x", -hop).astype(jnp.float32)
        total = total.astype(jnp.bfloat16)
        return total.astype(jnp.float32) + shift(total, "yh", 1).astype(jnp.float32)

    def whole(mine):
        theirs = shift(mine, "c", 1)
        first_core = place["c"] == 0
        return jnp.concatenate(
            (jnp.where(first_core, mine, theirs), jnp.where(first_core, theirs, mine))
        )

    gradient = reduced(gradient)
    squares = jnp.sum((gradient * gradient).reshape(-1, 8, hidden), axis=0)
    squares = squares + shift(squares, "c", 1)
    squares = squares + shift(squares, "yl", 1)
    squares = squares + shift(squares, "x", 1) + shift(squares, "x", -1) + shift(squares, "x", 2)
    others = [shift(squares, "z", hop) for hop in range(1, 8)]
    for other in others:
        squares = squares + other
    squares = jnp.sum(squares)
    gradient = whole(gradient)
    hessian_vector = whole(reduced(hessian_vector))
    return sophia_step(gradient, hessian_vector, probe, moment, curvature, squares)


def solution(mesh):
    fine = Mesh(mesh.devices.reshape(tuple(SIZES.values())), AXES)
    dp, fsdp = ("yh", "c"), ("yl", "z", "x")
    return jax.shard_map(
        local,
        mesh=fine,
        in_specs=(
            P(dp + fsdp, None),
            P(dp, fsdp),
            P(None, fsdp),
            P(None, fsdp),
            P(None, fsdp),
            P(None, fsdp),
        ),
        out_specs=(P(None, fsdp), P(None, fsdp), P(None, fsdp)),
        check_vma=False,
    )
```

```python
import functools

import jax
import jax.numpy as jnp
from jax import lax
from jax.experimental import pallas as pl
from jax.experimental.pallas import tpu as pltpu
from jax.sharding import Mesh, PartitionSpec as P

D = 2048
FF = 8192
HALF = D // 2
TOK = 128
HESS = 64
HID = 128
WIDE = 4 * HID
GROUP = 4 * TOK

inv_root_two = 0.7071067811865476
inv_root_tau = 0.3989422804014327
beta_first = 0.96
beta_second = 0.99
gamma_scale = 0.5
floor_value = 0.1

SIZES = {"yl": 2, "z": 8, "x": 4, "yh": 2, "c": 2}
AXES = tuple(SIZES)
HOPS = (0, 1, -1, 2)
CHUNKS = (
    ((0, 0), (0, -1), (0, 1), (1, 0)),
    ((0, -2), (0, 2), (1, -1), (0, -3)),
    ((0, 3), (1, -2), (0, -4), (1, 1)),
    ((1, -3), (1, -4), (1, 2), (1, 3)),
)

F32, BF16 = jnp.float32, jnp.bfloat16
VMEM, SMEM, ANY = pltpu.VMEM, pltpu.SMEM, pl.ANY


def gelu_slopes(values):
    density = jnp.exp(-0.5 * values * values) * inv_root_tau
    normal_cdf = 0.5 * (1.0 + lax.erf(values * inv_root_two))
    return (normal_cdf + values * density, density * (2.0 - values * values))


def shape(dims, dtype):
    return jax.ShapeDtypeStruct(dims, dtype)


def spec(space):
    return pl.BlockSpec(memory_space=space)


def params(mib):
    return pltpu.CompilerParams(vmem_limit_bytes=mib << 20)


def cost(flops, moved, transcendentals=0):
    return pl.CostEstimate(flops=flops, bytes_accessed=moved, transcendentals=transcendentals)


def shift(value, axis, by):
    n = SIZES[axis]
    return lax.ppermute(value, axis, [(i, (i + by) % n) for i in range(n)])


def gather_tokens(tokens):
    got = {(0, 0): tokens}
    got[0, -1] = shift(tokens, "z", 1)
    got[0, 1] = shift(tokens, "z", -1)
    got[1, 0] = shift(tokens, "yl", 1)
    got[0, -2] = shift(got[0, -1], "z", 1)
    got[0, 2] = shift(got[0, 1], "z", -1)
    got[1, -1] = shift(got[0, -1], "yl", 1)
    got[0, -3] = shift(got[0, -2], "z", 1)
    got[0, 3] = shift(got[0, 2], "z", -1)
    got[1, -2] = shift(got[0, -2], "yl", 1)
    got[0, -4] = shift(got[0, -3], "z", 1)
    got[1, 1] = shift(got[1, 0], "z", -1)
    got[1, -3] = shift(got[0, -3], "yl", 1)
    got[1, -4] = shift(got[1, -3], "z", 1)
    got[1, 2] = shift(got[1, 1], "z", -1)
    got[1, 3] = shift(got[0, 3], "yl", 1)
    return got


def weights_kernel(place, weight, bits, own, mine):
    own[:HID, :] = weight[...].T.astype(BF16)
    own[HID:, :] = (2 * bits[...] - 1).astype(F32).T.astype(BF16)
    mine[...] = own[:, pl.ds(pl.multiple_of(place[0] * HALF, HALF), HALF)]


def pack_weights(place, weight, bits):
    return pl.pallas_call(
        weights_kernel,
        out_shape=(shape((2 * HID, D), BF16), shape((2 * HID, HALF), BF16)),
        in_specs=[spec(SMEM), spec(VMEM), spec(VMEM)],
        out_specs=(spec(VMEM), spec(VMEM)),
        compiler_params=params(32),
        cost_estimate=cost(1 << 20, 4 << 20),
        name="pack_weights",
    )(place, weight, bits)


def cotangent_kernel(place, cotangent, *outs):
    x, z, yl = place[1], place[2], place[3]
    for hop, out in zip(HOPS, outs):
        for number, chunk in enumerate(CHUNKS):
            starts = []
            for other, dz in chunk:
                row = lax.rem(yl + other, 2) * 8 + lax.rem(z + (dz + 8), 8)
                starts.append((row * 4 + lax.rem(x + (hop + 4), 4)) * TOK)
            for part in range(2):
                for pair in range(2):
                    rows = [
                        cotangent[pl.ds(pl.multiple_of(start + part * HESS, HESS), HESS), :]
                        for start in starts[2 * pair : 2 * pair + 2]
                    ]
                    lane = number * GROUP + part * 2 * TOK + pair * TOK
                    out[:, lane : lane + TOK] = jnp.concatenate(rows, axis=0).T


def pack_cotangent(place, cotangent):
    return pl.pallas_call(
        cotangent_kernel,
        out_shape=(shape((HID, 4 * GROUP), BF16),) * 4,
        in_specs=[spec(SMEM), spec(VMEM)],
        out_specs=(spec(VMEM),) * 4,
        compiler_params=params(32),
        cost_estimate=cost(1 << 20, 4 << 20),
        name="pack_cotangent",
    )(place, cotangent)


def product(left, right):
    return lax.dot_general(left, right, (((1,), (0,)), ((), ())), preferred_element_type=F32)


def product_nt(left, right):
    return lax.dot_general(left, right, (((1,), (1,)), ((), ())), preferred_element_type=F32)


def slopes_of_chunk(number, core, blocks, own, mine, theirs, ups, xs, wt, up, pre, tangent, first, second, sems):
    token_copies = []
    for index, block in enumerate(blocks):
        for part in range(2):
            target = xs.at[pl.ds(part * 2 * TOK + index * HESS, HESS), :]
            token_copies.append((block.at[pl.ds(part * HESS, HESS), :], target, sems.at[0]))
    weight_copies = []
    for kind in range(2):
        weight_copies.append((own.at[pl.ds(kind * HID, HID), :], wt.at[pl.ds(kind * WIDE, HID), :], sems.at[1]))
        for index in range(3):
            rows = pl.ds(kind * WIDE + (index + 1) * HID, HID)
            for half, side in ((core, mine), (1 - core, theirs)):
                lanes = pl.ds(pl.multiple_of(half * HALF, HALF), HALF)
                weight_copies.append((side[index].at[pl.ds(kind * HID, HID), :], wt.at[rows, lanes], sems.at[1]))
    up_copies = []
    for index, source in enumerate(ups):
        lanes = pl.ds(number * GROUP, GROUP)
        up_copies.append((source.at[:, lanes], up.at[pl.ds(index * HID, HID), :], sems.at[2]))
    copies = [
        [pltpu.make_async_copy(*copy) for copy in some] for some in (token_copies, weight_copies, up_copies)
    ]
    for some in copies:
        for copy in some:
            copy.start()
    for some in copies:
        for copy in some:
            copy.wait()

    pre[:, : 2 * TOK] = product_nt(wt[:WIDE, :], xs[: 2 * TOK, :])
    tangent[...] = product_nt(wt[WIDE:, :], xs[: 2 * TOK, :])
    pre[:, 2 * TOK :] = product_nt(wt[:WIDE, :], xs[2 * TOK :, :])
    for row in range(0, WIDE, 64):
        rows = slice(row, row + 64)
        for part in range(2):
            lanes = slice(part * 2 * TOK, (part + 1) * 2 * TOK)
            slope, bend = gelu_slopes(pre[rows, lanes])
            upstream = up[rows, lanes].astype(F32)
            first[rows, lanes] = (upstream * slope).astype(BF16)
            if part == 0:
                second[rows, :] = (upstream * bend * tangent[rows, :]).astype(BF16)


def chunk_scratch():
    return [
        VMEM((GROUP, D), BF16),
        VMEM((2 * WIDE, D), BF16),
        VMEM((WIDE, GROUP), BF16),
        VMEM((WIDE, GROUP), F32),
        VMEM((WIDE, 2 * TOK), F32),
        VMEM((WIDE, GROUP), BF16),
    ]


def chunk_kernel(number, *refs):
    place, blocks, own, mine, theirs, ups = refs[0], refs[1:5], refs[5], refs[6:9], refs[9:12], refs[12:16]
    grad, hess, xs, wt, up, pre, tangent, first, second, grad_sum, hess_sum, sems, sum_sems = refs[-13:]
    core = place[0]
    if number:
        loads = [
            pltpu.make_async_copy(grad, grad_sum, sum_sems.at[0]),
            pltpu.make_async_copy(hess, hess_sum, sum_sems.at[1]),
        ]
        for load in loads:
            load.start()
    slopes_of_chunk(number, core, blocks, own, mine, theirs, ups, xs, wt, up, pre, tangent, first, second, sems)
    if number:
        for load in loads:
            load.wait()
    for column in range(0, D, 256):
        lanes = slice(column, column + 256)
        grad_part = product(first[...], xs[:, lanes])
        hess_part = product(second[...], xs[: 2 * TOK, lanes])
        if number:
            grad_part += grad_sum[:, lanes]
            hess_part += hess_sum[:, lanes]
        grad_sum[:, lanes] = grad_part
        hess_sum[:, lanes] = hess_part
    stores = [
        pltpu.make_async_copy(grad_sum, grad, sum_sems.at[0]),
        pltpu.make_async_copy(hess_sum, hess, sum_sems.at[1]),
    ]
    for store in stores:
        store.start()
    for store in stores:
        store.wait()


def add_chunk(number, place, blocks, weights, ups, sums):
    operands = (place, *blocks, *weights, *ups, *sums)
    first_sum = len(operands) - len(sums)
    return pl.pallas_call(
        functools.partial(chunk_kernel, number),
        out_shape=(shape((WIDE, D), F32),) * 2,
        in_specs=[spec(SMEM)] + [spec(ANY)] * (len(operands) - 1),
        out_specs=(spec(ANY),) * 2,
        scratch_shapes=chunk_scratch()
        + [
            VMEM((WIDE, 2 * TOK), BF16),
            VMEM((WIDE, D), F32),
            VMEM((WIDE, D), F32),
            pltpu.SemaphoreType.DMA((3,)),
            pltpu.SemaphoreType.DMA((2,)),
        ],
        input_output_aliases={first_sum: 0, first_sum + 1: 1} if sums else {},
        compiler_params=params(40),
        cost_estimate=cost(3 << 30, 20 << 20, 1 << 20),
        name="add_chunk_%d" % number,
    )(*operands)


def split_halves(core, total, keep, give, keep_sem):
    copy = pltpu.make_async_copy(
        total.at[:, pl.ds(pl.multiple_of(core * HALF, HALF), HALF)], keep, keep_sem.at[0]
    )
    copy.start()
    give[...] = total[:, pl.ds(pl.multiple_of((1 - core) * HALF, HALF), HALF)].astype(BF16)
    copy.wait()


def last_gradient_kernel(number, *refs):
    place, blocks, own, mine, theirs, ups, grad = refs[0], refs[1:5], refs[5], refs[6:9], refs[9:12], refs[12:16], refs[16]
    keep, give, second, xs, wt, up, pre, tangent, first, grad_sum, sems, sum_sems = refs[17:]
    core = place[0]
    load = pltpu.make_async_copy(grad, grad_sum, sum_sems.at[0])
    load.start()
    slopes_of_chunk(number, core, blocks, own, mine, theirs, ups, xs, wt, up, pre, tangent, first, second, sems)
    load.wait()
    for column in range(0, D, 256):
        lanes = slice(column, column + 256)
        grad_sum[:, lanes] += product(first[...], xs[:, lanes])
    split_halves(core, grad_sum, keep, give, sum_sems)


def last_gradient(number, place, blocks, weights, ups, grad):
    operands = (place, *blocks, *weights, *ups, grad)
    return pl.pallas_call(
        functools.partial(last_gradient_kernel, number),
        out_shape=(
            shape((WIDE, HALF), F32),
            shape((WIDE, HALF), BF16),
            shape((WIDE, 2 * TOK), BF16),
        ),
        in_specs=[spec(SMEM)] + [spec(ANY)] * (len(operands) - 1),
        out_specs=(spec(ANY), spec(VMEM), spec(VMEM)),
        scratch_shapes=chunk_scratch()
        + [
            VMEM((WIDE, D), F32),
            pltpu.SemaphoreType.DMA((3,)),
            pltpu.SemaphoreType.DMA((1,)),
        ],
        compiler_params=params(40),
        cost_estimate=cost(3 << 30, 20 << 20, 1 << 20),
        name="last_gradient",
    )(*operands)


def last_hessian_kernel(place, b0, b1, b2, b3, second, hess, keep, give, xs, hess_sum, sems):
    core = place[0]
    load = pltpu.make_async_copy(hess, hess_sum, sems.at[0])
    load.start()
    copies = [
        pltpu.make_async_copy(block.at[pl.ds(0, HESS), :], xs.at[pl.ds(index * HESS, HESS), :], sems.at[1])
        for index, block in enumerate((b0, b1, b2, b3))
    ]
    for copy in copies:
        copy.start()
    for copy in copies:
        copy.wait()
    load.wait()
    for column in range(0, D, 256):
        lanes = slice(column, column + 256)
        hess_sum[:, lanes] += product(second[...], xs[:, lanes])
    split_halves(core, hess_sum, keep, give, sems)


def last_hessian(place, blocks, second, hess):
    return pl.pallas_call(
        last_hessian_kernel,
        out_shape=(shape((WIDE, HALF), F32), shape((WIDE, HALF), BF16)),
        in_specs=[spec(SMEM)] + [spec(ANY)] * 4 + [spec(VMEM), spec(ANY)],
        out_specs=(spec(ANY), spec(VMEM)),
        scratch_shapes=[
            VMEM((2 * TOK, D), BF16),
            VMEM((WIDE, D), F32),
            pltpu.SemaphoreType.DMA((2,)),
        ],
        compiler_params=params(32),
        cost_estimate=cost(1 << 29, 8 << 20),
        name="last_hessian",
    )(place, *blocks, second, hess)


def sophia_step(gradient, hessian_vector, probe_bits, moment, curvature, squares):
    probe = (2 * probe_bits - 1).astype(F32)
    scale = jnp.minimum(1.0, lax.rsqrt(squares / (D * FF) + 1e-06))
    estimate = 2.0 * scale * probe * hessian_vector
    moment_out = beta_first * moment + (1.0 - beta_first) * scale * gradient
    curvature_out = beta_second * curvature + (1.0 - beta_second) * estimate
    update = jnp.clip(moment_out / jnp.maximum(gamma_scale * curvature_out, floor_value), -1.0, 1.0)
    return (moment_out, curvature_out, update)


def local(tokens, cotangent, weight, probe_bits, moment, curvature):
    place = jnp.stack([lax.axis_index(axis) for axis in ("c", "x", "z", "yl")]).astype(jnp.int32)
    core = lax.axis_index("c")

    got = gather_tokens(tokens)
    own, mine = pack_weights(place, weight, probe_bits)
    mine = [shift(mine, "x", hop) for hop in HOPS[1:]]
    theirs = [shift(part, "c", 1) for part in mine]
    weights = (own, *mine, *theirs)
    ups = pack_cotangent(place, cotangent)
    ups = [part if hop == 0 else shift(part, "x", hop) for hop, part in zip(HOPS, ups)]

    sums = ()
    for number, chunk in enumerate(CHUNKS[:-1]):
        sums = add_chunk(number, place, [got[key] for key in chunk], weights, ups, sums)
    blocks = [got[key] for key in CHUNKS[-1]]
    keep_grad, give_grad, second = last_gradient(3, place, blocks, weights, ups, sums[0])
    keep_hess, give_hess = last_hessian(place, blocks, second, sums[1])

    def reduced(keep, give):
        keep = keep + shift(give, "c", 1).astype(F32)
        total = keep[:HID]
        for number, hop in enumerate(HOPS):
            if number:
                sent = keep[number * HID : (number + 1) * HID].astype(BF16)
                total = total + shift(sent, "x", -hop).astype(F32)
        total = total.astype(BF16)
        return total.astype(F32) + shift(total, "yh", 1).astype(F32)

    def whole(mine):
        theirs = shift(mine, "c", 1)
        return jnp.concatenate(
            (jnp.where(core == 0, mine, theirs), jnp.where(core == 0, theirs, mine)), axis=1
        ).T

    gradient = reduced(keep_grad, give_grad)
    squares = jnp.sum((gradient * gradient).reshape(-1, 8, HALF // TOK, TOK), axis=(0, 2))
    squares = squares + shift(squares, "c", 1)
    squares = squares + shift(squares, "yl", 1)
    squares = squares + shift(squares, "x", 1) + shift(squares, "x", -1) + shift(squares, "x", 2)
    others = [shift(squares, "z", hop) for hop in range(1, 8)]
    for other in others:
        squares = squares + other
    squares = jnp.sum(squares)
    gradient = whole(gradient)
    hessian_vector = whole(reduced(keep_hess, give_hess))
    return sophia_step(gradient, hessian_vector, probe_bits, moment, curvature, squares)


def solution(mesh):
    fine = Mesh(mesh.devices.reshape(tuple(SIZES.values())), AXES)
    dp, fsdp = ("yh", "c"), ("yl", "z", "x")
    return jax.shard_map(
        local,
        mesh=fine,
        in_specs=(
            P(dp + fsdp, None),
            P(dp, fsdp),
            P(None, fsdp),
            P(None, fsdp),
            P(None, fsdp),
            P(None, fsdp),
        ),
        out_specs=(P(None, fsdp), P(None, fsdp), P(None, fsdp)),
        check_vma=False,
    )
```

```python
import functools

import jax
import jax.numpy as jnp
from jax import lax
from jax.experimental import pallas as pl
from jax.experimental.pallas import tpu as pltpu
from jax.sharding import Mesh, PartitionSpec as P

D = 2048
FF = 8192
HALF = D // 2
TOK = 128
HESS = 64
HID = 128
WIDE = 4 * HID
GROUP = 4 * TOK

inv_root_two = 0.7071067811865476
inv_root_tau = 0.3989422804014327
beta_first = 0.96
beta_second = 0.99
gamma_scale = 0.5
floor_value = 0.1

SIZES = {"yl": 2, "z": 8, "x": 4, "yh": 2, "c": 2}
AXES = tuple(SIZES)
HOPS = (0, 1, -1, 2)
CHUNKS = (
    ((0, 0), (0, -1), (0, 1), (1, 0)),
    ((0, -2), (0, 2), (1, -1), (0, -3)),
    ((0, 3), (1, -2), (0, -4), (1, 1)),
    ((1, -3), (1, -4), (1, 2), (1, 3)),
)

F32, BF16 = jnp.float32, jnp.bfloat16
VMEM, SMEM, ANY = pltpu.VMEM, pltpu.SMEM, pl.ANY


def gelu_slopes(values):
    density = jnp.exp(-0.5 * values * values) * inv_root_tau
    normal_cdf = 0.5 * (1.0 + lax.erf(values * inv_root_two))
    return (normal_cdf + values * density, density * (2.0 - values * values))


def shape(dims, dtype):
    return jax.ShapeDtypeStruct(dims, dtype)


def spec(space):
    return pl.BlockSpec(memory_space=space)


def params(mib):
    return pltpu.CompilerParams(vmem_limit_bytes=mib << 20)


def cost(flops, moved, transcendentals=0):
    return pl.CostEstimate(flops=flops, bytes_accessed=moved, transcendentals=transcendentals)


def shift(value, axis, by):
    n = SIZES[axis]
    with jax.named_scope("%s%d" % (axis, by)):
        return lax.ppermute(value, axis, [(i, (i + by) % n) for i in range(n)])


def after(values, done):
    return lax.optimization_barrier((values, done))


def weights_kernel(place, weight, bits, own, mine):
    own[:HID, :] = weight[...].T.astype(BF16)
    own[HID:, :] = (2 * bits[...] - 1).astype(F32).T.astype(BF16)
    mine[...] = own[:, pl.ds(pl.multiple_of(place[0] * HALF, HALF), HALF)]


def pack_weights(place, weight, bits):
    return pl.pallas_call(
        weights_kernel,
        out_shape=(shape((2 * HID, D), BF16), shape((2 * HID, HALF), BF16)),
        in_specs=[spec(SMEM), spec(VMEM), spec(VMEM)],
        out_specs=(spec(VMEM), spec(VMEM)),
        compiler_params=params(8),
        cost_estimate=cost(1 << 20, 4 << 20),
        name="pack_weights",
    )(place, weight, bits)


def join_kernel(first, second, third, fourth, out, sems):
    copies = []
    row = 0
    for index, part in enumerate((first, second, third, fourth)):
        rows = part.shape[0]
        copies.append(pltpu.make_async_copy(part, out.at[pl.ds(row, rows), :], sems.at[index]))
        row += rows
    for copy in copies:
        copy.start()
    for copy in copies:
        copy.wait()


def join(parts):
    return pl.pallas_call(
        join_kernel,
        out_shape=shape((6 * HID, HALF), BF16),
        in_specs=[spec(ANY)] * 4,
        out_specs=spec(ANY),
        scratch_shapes=[pltpu.SemaphoreType.DMA((4,))],
        compiler_params=params(4),
        cost_estimate=cost(0, 3 << 20),
        name="join",
    )(*parts)


def cotangent_kernel(place, cotangent, own, right, left):
    x, z, yl = place[1], place[2], place[3]
    for hop in HOPS:
        for number, chunk in enumerate(CHUNKS):
            starts = []
            for other, dz in chunk:
                row = lax.rem(yl + other, 2) * 8 + lax.rem(z + (dz + 8), 8)
                starts.append((row * 4 + lax.rem(x + (hop + 4), 4)) * TOK)
            for part in range(2):
                for pair in range(2):
                    rows = [
                        cotangent[pl.ds(pl.multiple_of(start + part * HESS, HESS), HESS), :]
                        for start in starts[2 * pair : 2 * pair + 2]
                    ]
                    turned = jnp.concatenate(rows, axis=0).T
                    lane = number * GROUP + part * 2 * TOK + pair * TOK
                    lanes = slice(lane, lane + TOK)
                    if hop == 2:
                        right[HID:, lanes] = turned[: HID // 2]
                        left[HID:, lanes] = turned[HID // 2 :]
                    else:
                        out = {0: own, 1: right, -1: left}[hop]
                        out[:HID, lanes] = turned


def pack_cotangent(place, cotangent):
    sent = shape((HID + HID // 2, 4 * GROUP), BF16)
    return pl.pallas_call(
        cotangent_kernel,
        out_shape=(shape((HID, 4 * GROUP), BF16), sent, sent),
        in_specs=[spec(SMEM), spec(VMEM)],
        out_specs=(spec(VMEM),) * 3,
        compiler_params=params(10),
        cost_estimate=cost(1 << 20, 4 << 20),
        name="pack_cotangent",
    )(place, cotangent)


def product(left, right):
    return lax.dot_general(left, right, (((1,), (0,)), ((), ())), preferred_element_type=F32)


def product_nt(left, right):
    return lax.dot_general(left, right, (((1,), (1,)), ((), ())), preferred_element_type=F32)


def token_copies(blocks, xs, base, sem):
    return [
        pltpu.make_async_copy(
            block.at[pl.ds(part * HESS, HESS), :],
            xs.at[pl.ds(base + part * 2 * TOK + index * HESS, HESS), :],
            sem,
        )
        for index, block in enumerate(blocks)
        for part in range(2)
    ]


def weight_copies(core, own, mine, theirs, wt, sem):
    copies = []
    for kind in range(2):
        copies.append(pltpu.make_async_copy(own.at[pl.ds(kind * HID, HID), :], wt.at[pl.ds(kind * WIDE, HID), :], sem))
        for index in range(3):
            start_row = index * 2 * HID + kind * HID
            rows = pl.ds(kind * WIDE + (index + 1) * HID, HID)
            source = mine[index].at[pl.ds(kind * HID, HID), :] if index < 2 else mine[2 + kind]
            lanes = pl.ds(pl.multiple_of(core * HALF, HALF), HALF)
            copies.append(pltpu.make_async_copy(source, wt.at[rows, lanes], sem))
            lanes = pl.ds(pl.multiple_of((1 - core) * HALF, HALF), HALF)
            copies.append(pltpu.make_async_copy(theirs.at[pl.ds(start_row, HID), :], wt.at[rows, lanes], sem))
    return copies


def upstream_copies(number, ups, up, sem):
    own, right, left, low, high = ups
    lanes, to = pl.ds(number * GROUP, GROUP), pl.ds(0, GROUP)
    half = HID // 2
    return [
        pltpu.make_async_copy(own.at[:, lanes], up.at[pl.ds(0, HID), to], sem),
        pltpu.make_async_copy(right.at[pl.ds(0, HID), lanes], up.at[pl.ds(HID, HID), to], sem),
        pltpu.make_async_copy(left.at[pl.ds(0, HID), lanes], up.at[pl.ds(2 * HID, HID), to], sem),
        pltpu.make_async_copy(low.at[:, lanes], up.at[pl.ds(3 * HID, half), to], sem),
        pltpu.make_async_copy(high.at[:, lanes], up.at[pl.ds(3 * HID + half, half), to], sem),
    ]


def start(copies):
    for copy in copies:
        copy.start()


def wait(copies):
    for copy in copies:
        copy.wait()


ROWS = [slice(row, row + 64) for row in range(0, WIDE, 64)]
PARTS = [slice(0, 2 * TOK), slice(2 * TOK, GROUP)]


def slopes_kernel(place, b0, b1, b2, b3, own, m0, m1, m2, m3, theirs, slope, curve, xs, wt, pre, tangent, sems):
    tokens = token_copies((b0, b1, b2, b3), xs, 0, sems.at[0])
    weights = weight_copies(place[0], own, (m0, m1, m2, m3), theirs, wt, sems.at[1])
    start(tokens)
    start(weights)
    wait(tokens)
    wait(weights)
    pre[:, PARTS[0]] = product_nt(wt[:WIDE, :], xs[PARTS[0], :])
    tangent[...] = product_nt(wt[WIDE:, :], xs[PARTS[0], :])
    pre[:, PARTS[1]] = product_nt(wt[:WIDE, :], xs[PARTS[1], :])
    for rows in ROWS:
        for part, lanes in enumerate(PARTS):
            one, two = gelu_slopes(pre[rows, lanes])
            slope[rows, lanes] = one
            if part == 0:
                curve[rows, :] = two * tangent[rows, :]


def slopes(place, blocks, weights):
    return pl.pallas_call(
        slopes_kernel,
        out_shape=(shape((WIDE, GROUP), F32), shape((WIDE, 2 * TOK), F32)),
        in_specs=[spec(SMEM)] + [spec(ANY)] * 10,
        out_specs=(spec(VMEM),) * 2,
        scratch_shapes=[
            VMEM((GROUP, D), BF16),
            VMEM((2 * WIDE, D), BF16),
            VMEM((WIDE, GROUP), F32),
            VMEM((WIDE, 2 * TOK), F32),
            pltpu.SemaphoreType.DMA((2,)),
        ],
        compiler_params=params(14),
        cost_estimate=cost(3 << 29, 8 << 20, 1 << 19),
        name="slopes",
    )(place, *blocks, *weights)


def products_kernel(chunks, *refs):
    blocks, ups = refs[: 4 * chunks], refs[4 * chunks : 4 * chunks + 5]
    factors = refs[4 * chunks + 5 : 6 * chunks + 5]
    grad, hess, xs, up, slope, curve, first, second, grad_sum, hess_sum, sems, store_sems = refs[6 * chunks + 5 :]
    loads = []
    for number in range(chunks):
        load = [
            pltpu.make_async_copy(factors[2 * number], slope.at[number], sems.at[number]),
            pltpu.make_async_copy(factors[2 * number + 1], curve.at[number], sems.at[number]),
        ] + upstream_copies(number, ups, up.at[number], sems.at[number])
        start(load)
        loads.append(load)
    tokens = []
    for number in range(chunks):
        tokens += token_copies(blocks[4 * number : 4 * number + 4], xs, number * GROUP, sems.at[chunks])
    start(tokens)
    for number in range(chunks):
        wait(loads[number])
        for rows in ROWS:
            for part, lanes in enumerate(PARTS):
                upstream = up[number, rows, lanes].astype(F32)
                first[rows, number * GROUP + lanes.start : number * GROUP + lanes.stop] = (
                    upstream * slope[number, rows, lanes]
                ).astype(BF16)
                if part == 0:
                    second[rows, number * 2 * TOK : (number + 1) * 2 * TOK] = (
                        upstream * curve[number, rows, :]
                    ).astype(BF16)
    wait(tokens)
    stores = []
    for column in range(0, D, 256):
        lanes = slice(column, column + 256)
        grad_sum[:, lanes] = product(first[...], xs[:, lanes])
        part = product(second[:, : 2 * TOK], xs[: 2 * TOK, lanes])
        for number in range(1, chunks):
            part += product(
                second[:, number * 2 * TOK : (number + 1) * 2 * TOK],
                xs[number * GROUP : number * GROUP + 2 * TOK, lanes],
            )
        hess_sum[:, lanes] = part
        where = pl.ds(column, 256)
        store = [
            pltpu.make_async_copy(grad_sum.at[:, where], grad.at[:, where], store_sems.at[0]),
            pltpu.make_async_copy(hess_sum.at[:, where], hess.at[:, where], store_sems.at[1]),
        ]
        start(store)
        stores += store
    wait(stores)


def products(blocks, ups, factors):
    chunks = len(factors) // 2
    operands = (*blocks, *ups, *factors)
    return pl.pallas_call(
        functools.partial(products_kernel, chunks),
        out_shape=(shape((WIDE, D), F32),) * 2,
        in_specs=[spec(ANY)] * len(operands),
        out_specs=(spec(ANY),) * 2,
        scratch_shapes=[
            VMEM((chunks * GROUP, D), BF16),
            VMEM((chunks, WIDE, GROUP), BF16),
            VMEM((chunks, WIDE, GROUP), F32),
            VMEM((chunks, WIDE, 2 * TOK), F32),
            VMEM((WIDE, chunks * GROUP), BF16),
            VMEM((WIDE, chunks * 2 * TOK), BF16),
            VMEM((WIDE, D), F32),
            VMEM((WIDE, D), F32),
            pltpu.SemaphoreType.DMA((chunks + 1,)),
            pltpu.SemaphoreType.DMA((2,)),
        ],
        compiler_params=params(28),
        cost_estimate=cost(5 << 30, 24 << 20),
        name="products",
    )(*operands)


def split_halves(core, total, keep, give, keep_sem):
    copy = pltpu.make_async_copy(
        total.at[:, pl.ds(pl.multiple_of(core * HALF, HALF), HALF)], keep, keep_sem
    )
    copy.start()
    give[...] = total[:, pl.ds(pl.multiple_of((1 - core) * HALF, HALF), HALF)].astype(BF16)
    copy.wait()


def last_gradient_kernel(number, *refs):
    place, blocks, own, mine, theirs, ups, grad = refs[0], refs[1:5], refs[5], refs[6:10], refs[10], refs[11:16], refs[16]
    keep, give, second, xs, wt, up, pre, tangent, first, grad_sum, sems = refs[17:]
    core = place[0]
    tokens = token_copies(blocks, xs, 0, sems.at[0])
    weights = weight_copies(core, own, mine, theirs, wt, sems.at[1])
    upstreams = upstream_copies(number, ups, up, sems.at[2])
    load = pltpu.make_async_copy(grad, grad_sum, sems.at[3])
    start(tokens)
    start(weights)
    start(upstreams)
    load.start()
    wait(tokens)
    wait(weights)
    wait(upstreams)
    pre[:, PARTS[0]] = product_nt(wt[:WIDE, :], xs[PARTS[0], :])
    tangent[...] = product_nt(wt[WIDE:, :], xs[PARTS[0], :])
    pre[:, PARTS[1]] = product_nt(wt[:WIDE, :], xs[PARTS[1], :])
    for rows in ROWS:
        for part, lanes in enumerate(PARTS):
            slope, bend = gelu_slopes(pre[rows, lanes])
            upstream = up[rows, lanes].astype(F32)
            first[rows, lanes] = (upstream * slope).astype(BF16)
            if part == 0:
                second[rows, :] = (upstream * (bend * tangent[rows, :])).astype(BF16)
    load.wait()
    for column in range(0, D, 256):
        lanes = slice(column, column + 256)
        grad_sum[:, lanes] += product(first[...], xs[:, lanes])
    split_halves(core, grad_sum, keep, give, sems.at[0])


def last_gradient(number, place, blocks, weights, ups, grad):
    operands = (place, *blocks, *weights, *ups, grad)
    return pl.pallas_call(
        functools.partial(last_gradient_kernel, number),
        out_shape=(
            shape((WIDE, HALF), F32),
            shape((WIDE, HALF), BF16),
            shape((WIDE, 2 * TOK), BF16),
        ),
        in_specs=[spec(SMEM)] + [spec(ANY)] * (len(operands) - 1),
        out_specs=(spec(ANY), spec(VMEM), spec(VMEM)),
        scratch_shapes=[
            VMEM((GROUP, D), BF16),
            VMEM((2 * WIDE, D), BF16),
            VMEM((WIDE, GROUP), BF16),
            VMEM((WIDE, GROUP), F32),
            VMEM((WIDE, 2 * TOK), F32),
            VMEM((WIDE, GROUP), BF16),
            VMEM((WIDE, D), F32),
            pltpu.SemaphoreType.DMA((4,)),
        ],
        compiler_params=params(20),
        cost_estimate=cost(5 << 29, 12 << 20, 1 << 19),
        name="last_gradient",
    )(*operands)


def last_hessian_kernel(place, b0, b1, b2, b3, second, hess, keep, give, xs, hess_sum, sems):
    core = place[0]
    load = pltpu.make_async_copy(hess, hess_sum, sems.at[0])
    load.start()
    copies = [
        pltpu.make_async_copy(block.at[pl.ds(0, HESS), :], xs.at[pl.ds(index * HESS, HESS), :], sems.at[1])
        for index, block in enumerate((b0, b1, b2, b3))
    ]
    for copy in copies:
        copy.start()
    for copy in copies:
        copy.wait()
    load.wait()
    for column in range(0, D, 256):
        lanes = slice(column, column + 256)
        hess_sum[:, lanes] += product(second[...], xs[:, lanes])
    split_halves(core, hess_sum, keep, give, sems.at[0])


def last_hessian(place, blocks, second, hess):
    return pl.pallas_call(
        last_hessian_kernel,
        out_shape=(shape((WIDE, HALF), F32), shape((WIDE, HALF), BF16)),
        in_specs=[spec(SMEM)] + [spec(ANY)] * 4 + [spec(VMEM), spec(ANY)],
        out_specs=(spec(ANY), spec(VMEM)),
        scratch_shapes=[
            VMEM((2 * TOK, D), BF16),
            VMEM((WIDE, D), F32),
            pltpu.SemaphoreType.DMA((2,)),
        ],
        compiler_params=params(10),
        cost_estimate=cost(1 << 29, 8 << 20),
        name="last_hessian",
    )(place, *blocks, second, hess)


def sophia_kernel(place, grad_mine, grad_theirs, hess_mine, hess_theirs, bits, moment, curvature, s0, s1, s2, s3, *refs):
    outs, stage, sems = refs[:3], refs[3:6], refs[6]
    core = place[0]
    squares = jnp.sum((s0[...] + s1[...]) + (s2[...] + s3[...]))
    scale = jnp.minimum(1.0, lax.rsqrt(squares / (D * FF) + 1e-06))
    copies = []
    for half, grad, hess in ((core, grad_mine, hess_mine), (1 - core, grad_theirs, hess_theirs)):
        for part in range(4):
            lanes = slice(part * 256, (part + 1) * 256)
            rows = pl.ds(pl.multiple_of(half * HALF + part * 256, 256), 256)
            probe = (2 * bits[rows, :] - 1).astype(F32)
            estimate = 2.0 * scale * probe * hess[:, lanes].T
            moment_out = beta_first * moment[rows, :] + (1.0 - beta_first) * scale * grad[:, lanes].T
            curvature_out = beta_second * curvature[rows, :] + (1.0 - beta_second) * estimate
            stage[0][rows, :] = moment_out
            stage[1][rows, :] = curvature_out
            stage[2][rows, :] = jnp.clip(
                moment_out / jnp.maximum(gamma_scale * curvature_out, floor_value), -1.0, 1.0
            )
            for index in range(3):
                copy = pltpu.make_async_copy(stage[index].at[rows, :], outs[index].at[rows, :], sems.at[index])
                copy.start()
                copies.append(copy)
    wait(copies)


def sophia_step(place, sums, state, squares):
    return pl.pallas_call(
        sophia_kernel,
        out_shape=(shape((D, HID), F32),) * 3,
        in_specs=[spec(SMEM)] + [spec(VMEM)] * 11,
        out_specs=(spec(ANY),) * 3,
        scratch_shapes=[VMEM((D, HID), F32)] * 3 + [pltpu.SemaphoreType.DMA((3,))],
        compiler_params=params(14),
        cost_estimate=cost(1 << 23, 8 << 20),
        name="sophia_step",
    )(place, *sums, *state, *squares)


def four(value, axes, pairs):
    return [value] + [lax.ppermute(value, axes, pair) for pair in pairs]


YL_Z = (
    ("yl", "z"),
    [
        [(y * 8 + z, (y ^ dy) * 8 + (z ^ dz)) for y in range(2) for z in range(8)]
        for dy, dz in ((1, 0), (0, 1), (1, 1))
    ],
)
Z = ("z", [[(z, (z + by) % 8) for z in range(8)] for by in (2, 6, 4)])
X = ("x", [[(x, (x + by) % 4) for x in range(4)] for by in (1, 3, 2)])


def local(tokens, cotangent, weight, probe_bits, moment, curvature):
    place = jnp.stack([lax.axis_index(axis) for axis in ("c", "x", "z", "yl")]).astype(jnp.int32)
    core = lax.axis_index("c")

    got = {(0, 0): tokens}
    got[0, -1] = shift(tokens, "z", 1)
    got[0, 1] = shift(tokens, "z", -1)
    got[1, 0] = shift(tokens, "yl", 1)
    own, sent = pack_weights(place, weight, probe_bits)
    right, left = shift(sent, "x", 1), shift(sent, "x", -1)

    place, (got[0, -1], got[0, 1], got[1, 0]) = after(place, (got[0, -1], got[0, 1], got[1, 0]))
    got[0, -2] = shift(got[0, -1], "z", 1)
    got[0, 2] = shift(got[0, 1], "z", -1)
    got[1, -1] = shift(got[0, -1], "yl", 1)
    mine = [right, left, shift(right[:HID], "x", 1), shift(left[HID:], "x", -1)]
    turned = pack_cotangent(place, cotangent)

    (mine, turned), (got[0, -2], got[0, 2], got[1, -1]) = after((mine, turned), (got[0, -2], got[0, 2], got[1, -1]))
    got[0, -3] = shift(got[0, -2], "z", 1)
    got[0, 3] = shift(got[0, 2], "z", -1)
    got[1, -2] = shift(got[0, -2], "yl", 1)
    theirs, turned = after(shift(join(mine), "c", 1), turned)
    right, left = shift(turned[1], "x", 1), shift(turned[2], "x", -1)
    weights = (own, *mine, theirs)
    factors = [*slopes(place, [got[key] for key in CHUNKS[0]], weights)]

    factors, (got[0, -3], got[0, 3], got[1, -2]) = after(factors, (got[0, -3], got[0, 3], got[1, -2]))
    got[0, -4] = shift(got[0, -3], "z", 1)
    got[1, 1] = shift(got[1, 0], "z", -1)
    got[1, -3] = shift(got[0, -3], "yl", 1)
    ups = [turned[0], right, left, shift(right[HID:], "x", 1), shift(left[HID:], "x", -1)]
    factors += slopes(place, [got[key] for key in CHUNKS[1]], weights)

    factors, (got[0, -4], got[1, 1], got[1, -3]) = after(factors, (got[0, -4], got[1, 1], got[1, -3]))
    got[1, -4] = shift(got[1, -3], "z", 1)
    got[1, 2] = shift(got[1, 1], "z", -1)
    got[1, 3] = shift(got[0, 3], "yl", 1)
    factors += slopes(place, [got[key] for key in CHUNKS[2]], weights)
    grad, hess = products([got[key] for chunk in CHUNKS[:3] for key in chunk], ups, factors)

    (grad, hess), (got[1, -4], got[1, 2], got[1, 3]) = after((grad, hess), (got[1, -4], got[1, 2], got[1, 3]))
    blocks = [got[key] for key in CHUNKS[3]]
    keep_grad, give_grad, second = last_gradient(3, place, blocks, weights, ups, grad)
    keep_hess, give_hess = last_hessian(place, blocks, second, hess)

    def over_cores(keep, give):
        keep = keep + shift(give, "c", 1).astype(F32)
        return keep[:HID], [keep[n * HID : (n + 1) * HID].astype(BF16) for n in range(1, 4)]

    def add_x(total, parts):
        for part in parts:
            total = total + part.astype(F32)
        return total.astype(BF16)

    def over_y(total):
        return total.astype(F32) + shift(total, "yh", 1).astype(F32)

    grad_own, grad_sent = over_cores(keep_grad, give_grad)
    hess_own, hess_sent = over_cores(keep_hess, give_hess)
    gradient = add_x(grad_own, [shift(part, "x", -hop) for hop, part in zip(HOPS[1:], grad_sent)])
    hess_sent[2], gradient = after(hess_sent[2], gradient)
    gradient, far = after(over_y(gradient), shift(hess_sent[2], "x", -HOPS[3]))
    gradients, hess_sent = after((gradient, shift(gradient, "c", 1)), hess_sent)
    squares = [jnp.sum((half * half).reshape(-1, 8, HALF // TOK, TOK), axis=(0, 2)) for half in gradients]
    squares = sum(four(squares[0] + squares[1], *YL_Z))
    near = [shift(part, "x", -hop) for hop, part in zip(HOPS[1:3], hess_sent)]
    hessian_vector, squares = after(add_x(hess_own, (*near, far)), squares)
    hessian_vector, squares = after(over_y(hessian_vector), sum(four(squares, *Z)))
    return sophia_step(
        place,
        (*gradients, hessian_vector, shift(hessian_vector, "c", 1)),
        (probe_bits, moment, curvature),
        four(squares, *X),
    )


def solution(mesh):
    fine = Mesh(mesh.devices.reshape(tuple(SIZES.values())), AXES)
    dp, fsdp = ("yh", "c"), ("yl", "z", "x")
    return jax.shard_map(
        local,
        mesh=fine,
        in_specs=(
            P(dp + fsdp, None),
            P(dp, fsdp),
            P(None, fsdp),
            P(None, fsdp),
            P(None, fsdp),
            P(None, fsdp),
        ),
        out_specs=(P(None, fsdp), P(None, fsdp), P(None, fsdp)),
        check_vma=False,
    )
```

```python
import functools

import jax
import jax.numpy as jnp
from jax import lax
from jax.experimental import pallas as pl
from jax.experimental.pallas import tpu as pltpu
from jax.sharding import Mesh, PartitionSpec as P

D = 2048
FF = 8192
HALF = D // 2
TOK = 128
HESS = 64
HID = 128
WIDE = 4 * HID
GROUP = 4 * TOK

inv_root_two = 0.7071067811865476
inv_root_tau = 0.3989422804014327
beta_first = 0.96
beta_second = 0.99
gamma_scale = 0.5
floor_value = 0.1

SIZES = {"yl": 2, "z": 8, "x": 4, "yh": 2, "c": 2}
AXES = tuple(SIZES)
HOPS = (0, 1, -1, 2)
CHUNKS = (
    ((0, 0), (0, -1), (0, 1), (1, 0)),
    ((0, -2), (0, 2), (1, -1), (0, -3)),
    ((0, 3), (1, -2), (0, -4), (1, 1)),
    ((1, -3), (1, -4), (1, 2), (1, 3)),
)

F32, BF16 = jnp.float32, jnp.bfloat16
VMEM, SMEM, ANY = pltpu.VMEM, pltpu.SMEM, pl.ANY


def gelu_slopes(values):
    density = jnp.exp(-0.5 * values * values) * inv_root_tau
    normal_cdf = 0.5 * (1.0 + lax.erf(values * inv_root_two))
    return (normal_cdf + values * density, density * (2.0 - values * values))


def shape(dims, dtype):
    return jax.ShapeDtypeStruct(dims, dtype)


def spec(space):
    return pl.BlockSpec(memory_space=space)


def params(mib):
    return pltpu.CompilerParams(vmem_limit_bytes=mib << 20)


def cost(flops, moved, transcendentals=0):
    return pl.CostEstimate(flops=flops, bytes_accessed=moved, transcendentals=transcendentals)


def shift(value, axis, by):
    n = SIZES[axis]
    with jax.named_scope("%s%d" % (axis, by)):
        return lax.ppermute(value, axis, [(i, (i + by) % n) for i in range(n)])


def after(values, done):
    return lax.optimization_barrier((values, done))


def weights_kernel(place, weight, bits, own, mine, weight_in, bits_in, sems):
    parts = 4
    copies = []
    for part in range(parts):
        rows = pl.ds(part * (D // parts), D // parts)
        copies.append(
            [
                pltpu.make_async_copy(weight.at[rows, :], weight_in.at[rows, :], sems.at[part]),
                pltpu.make_async_copy(bits.at[rows, :], bits_in.at[rows, :], sems.at[part]),
            ]
        )
        for copy in copies[-1]:
            copy.start()
    for part in range(parts):
        for copy in copies[part]:
            copy.wait()
        rows = slice(part * (D // parts), (part + 1) * (D // parts))
        own[:HID, rows] = weight_in[rows, :].T.astype(BF16)
        own[HID:, rows] = (2 * bits_in[rows, :] - 1).astype(F32).T.astype(BF16)
    mine[...] = own[:, pl.ds(pl.multiple_of(place[0] * HALF, HALF), HALF)]


def pack_weights(place, weight, bits):
    return pl.pallas_call(
        weights_kernel,
        out_shape=(shape((2 * HID, D), BF16), shape((2 * HID, HALF), BF16)),
        in_specs=[spec(SMEM), spec(ANY), spec(ANY)],
        out_specs=(spec(VMEM), spec(VMEM)),
        scratch_shapes=[VMEM((D, HID), F32), VMEM((D, HID), jnp.int32), pltpu.SemaphoreType.DMA((4,))],
        compiler_params=params(8),
        cost_estimate=cost(1 << 20, 4 << 20),
        name="pack_weights",
    )(place, weight, bits)


def join_kernel(first, second, third, fourth, out, sems):
    copies = []
    row = 0
    for index, part in enumerate((first, second, third, fourth)):
        rows = part.shape[0]
        copies.append(pltpu.make_async_copy(part, out.at[pl.ds(row, rows), :], sems.at[index]))
        row += rows
    for copy in copies:
        copy.start()
    for copy in copies:
        copy.wait()


def join(parts):
    return pl.pallas_call(
        join_kernel,
        out_shape=shape((6 * HID, HALF), BF16),
        in_specs=[spec(ANY)] * 4,
        out_specs=spec(ANY),
        scratch_shapes=[pltpu.SemaphoreType.DMA((4,))],
        compiler_params=params(4),
        cost_estimate=cost(0, 3 << 20),
        name="join",
    )(*parts)


def cotangent_kernel(place, cotangent, own, right, left):
    x, z, yl = place[1], place[2], place[3]
    for hop in HOPS:
        for number, chunk in enumerate(CHUNKS):
            starts = []
            for other, dz in chunk:
                row = lax.rem(yl + other, 2) * 8 + lax.rem(z + (dz + 8), 8)
                starts.append((row * 4 + lax.rem(x + (hop + 4), 4)) * TOK)
            for part in range(2):
                for pair in range(2):
                    rows = [
                        cotangent[pl.ds(pl.multiple_of(start + part * HESS, HESS), HESS), :]
                        for start in starts[2 * pair : 2 * pair + 2]
                    ]
                    turned = jnp.concatenate(rows, axis=0).T
                    lane = number * GROUP + part * 2 * TOK + pair * TOK
                    lanes = slice(lane, lane + TOK)
                    if hop == 2:
                        right[HID:, lanes] = turned[: HID // 2]
                        left[HID:, lanes] = turned[HID // 2 :]
                    else:
                        out = {0: own, 1: right, -1: left}[hop]
                        out[:HID, lanes] = turned


def pack_cotangent(place, cotangent):
    sent = shape((HID + HID // 2, 4 * GROUP), BF16)
    return pl.pallas_call(
        cotangent_kernel,
        out_shape=(shape((HID, 4 * GROUP), BF16), sent, sent),
        in_specs=[spec(SMEM), spec(VMEM)],
        out_specs=(spec(VMEM),) * 3,
        compiler_params=params(10),
        cost_estimate=cost(1 << 20, 4 << 20),
        name="pack_cotangent",
    )(place, cotangent)


def product(left, right):
    return lax.dot_general(left, right, (((1,), (0,)), ((), ())), preferred_element_type=F32)


def product_nt(left, right):
    return lax.dot_general(left, right, (((1,), (1,)), ((), ())), preferred_element_type=F32)


def token_copies(blocks, xs, base, sem):
    return [
        pltpu.make_async_copy(
            block.at[pl.ds(part * HESS, HESS), :],
            xs.at[pl.ds(base + part * 2 * TOK + index * HESS, HESS), :],
            sem,
        )
        for index, block in enumerate(blocks)
        for part in range(2)
    ]


def weight_copies(core, own, mine, theirs, wt, sem):
    copies = []
    for kind in range(2):
        copies.append(pltpu.make_async_copy(own.at[pl.ds(kind * HID, HID), :], wt.at[pl.ds(kind * WIDE, HID), :], sem))
        for index in range(3):
            start_row = index * 2 * HID + kind * HID
            rows = pl.ds(kind * WIDE + (index + 1) * HID, HID)
            source = mine[index].at[pl.ds(kind * HID, HID), :] if index < 2 else mine[2 + kind]
            lanes = pl.ds(pl.multiple_of(core * HALF, HALF), HALF)
            copies.append(pltpu.make_async_copy(source, wt.at[rows, lanes], sem))
            lanes = pl.ds(pl.multiple_of((1 - core) * HALF, HALF), HALF)
            copies.append(pltpu.make_async_copy(theirs.at[pl.ds(start_row, HID), :], wt.at[rows, lanes], sem))
    return copies


def upstream_rows(ups, number, index, lanes):
    own, right, left, low, high = ups
    source, row = ((own, 0), (own, 64), (right, 0), (right, 64), (left, 0), (left, 64), (low, 0), (high, 0))[index]
    return source[row : row + 64, number * GROUP + lanes.start : number * GROUP + lanes.stop].astype(F32)


def start(copies):
    for copy in copies:
        copy.start()


def wait(copies):
    for copy in copies:
        copy.wait()


ROWS = [slice(row, row + 64) for row in range(0, WIDE, 64)]
PARTS = [slice(0, 2 * TOK), slice(2 * TOK, GROUP)]


def slopes_kernel(place, b0, b1, b2, b3, own, m0, m1, m2, m3, theirs, slope, curve, xs, wt, pre, tangent, sems):
    tokens = token_copies((b0, b1, b2, b3), xs, 0, sems.at[0])
    weights = weight_copies(place[0], own, (m0, m1, m2, m3), theirs, wt, sems.at[1])
    start(tokens)
    start(weights)
    wait(tokens)
    wait(weights)
    pre[:, PARTS[0]] = product_nt(wt[:WIDE, :], xs[PARTS[0], :])
    tangent[...] = product_nt(wt[WIDE:, :], xs[PARTS[0], :])
    pre[:, PARTS[1]] = product_nt(wt[:WIDE, :], xs[PARTS[1], :])
    for rows in ROWS:
        for part, lanes in enumerate(PARTS):
            one, two = gelu_slopes(pre[rows, lanes])
            slope[rows, lanes] = one
            if part == 0:
                curve[rows, :] = two * tangent[rows, :]


def slopes(place, blocks, weights):
    return pl.pallas_call(
        slopes_kernel,
        out_shape=(shape((WIDE, GROUP), F32), shape((WIDE, 2 * TOK), F32)),
        in_specs=[spec(SMEM)] + [spec(ANY)] * 10,
        out_specs=(spec(VMEM),) * 2,
        scratch_shapes=[
            VMEM((GROUP, D), BF16),
            VMEM((2 * WIDE, D), BF16),
            VMEM((WIDE, GROUP), F32),
            VMEM((WIDE, 2 * TOK), F32),
            pltpu.SemaphoreType.DMA((2,)),
        ],
        compiler_params=params(14),
        cost_estimate=cost(3 << 29, 8 << 20, 1 << 19),
        name="slopes",
    )(place, *blocks, *weights)


def products_kernel(chunks, *refs):
    blocks, ups = refs[: 4 * chunks], refs[4 * chunks : 4 * chunks + 5]
    factors = refs[4 * chunks + 5 : 6 * chunks + 5]
    grad, hess, xs, first, second, sems = refs[6 * chunks + 5 :]
    tokens = []
    for number in range(chunks):
        tokens += token_copies(blocks[4 * number : 4 * number + 4], xs, number * GROUP, sems.at[0])
    start(tokens)
    for number in range(chunks):
        slope, curve = factors[2 * number : 2 * number + 2]
        for index, rows in enumerate(ROWS):
            for part, lanes in enumerate(PARTS):
                upstream = upstream_rows(ups, number, index, lanes)
                first[rows, number * GROUP + lanes.start : number * GROUP + lanes.stop] = (
                    upstream * slope[rows, lanes]
                ).astype(BF16)
                if part == 0:
                    second[rows, number * 2 * TOK : (number + 1) * 2 * TOK] = (upstream * curve[rows, :]).astype(BF16)
    wait(tokens)
    for column in range(0, D, 256):
        lanes = slice(column, column + 256)
        grad[:, lanes] = product(first[...], xs[:, lanes])
        part = product(second[:, : 2 * TOK], xs[: 2 * TOK, lanes])
        for number in range(1, chunks):
            part += product(
                second[:, number * 2 * TOK : (number + 1) * 2 * TOK],
                xs[number * GROUP : number * GROUP + 2 * TOK, lanes],
            )
        hess[:, lanes] = part


def products(blocks, ups, factors):
    chunks = len(factors) // 2
    operands = (*blocks, *ups, *factors)
    return pl.pallas_call(
        functools.partial(products_kernel, chunks),
        out_shape=(shape((WIDE, D), F32),) * 2,
        in_specs=[spec(ANY)] * len(blocks) + [spec(VMEM)] * (len(operands) - len(blocks)),
        out_specs=(spec(VMEM),) * 2,
        scratch_shapes=[
            VMEM((chunks * GROUP, D), BF16),
            VMEM((WIDE, chunks * GROUP), BF16),
            VMEM((WIDE, chunks * 2 * TOK), BF16),
            pltpu.SemaphoreType.DMA((1,)),
        ],
        compiler_params=params(30),
        cost_estimate=cost(5 << 30, 24 << 20),
        name="products",
    )(*operands)


def halves(core):
    tiles = []
    for half in range(2):
        base = (core if half == 0 else 1 - core) * HALF
        for column in range(0, HALF, 256):
            tiles.append((half, slice(column, column + 256), pl.ds(pl.multiple_of(base + column, 256), 256)))
    return tiles


def last_gradient_kernel(number, *refs):
    place, blocks, own, mine, theirs, ups, grad = refs[0], refs[1:5], refs[5], refs[6:10], refs[10], refs[11:16], refs[16]
    keep, give, second, xs, wt, pre, tangent, first, sems = refs[17:]
    core = place[0]
    tokens = token_copies(blocks, xs, 0, sems.at[0])
    weights = weight_copies(core, own, mine, theirs, wt, sems.at[1])
    start(tokens)
    start(weights)
    wait(tokens)
    wait(weights)
    pre[:, PARTS[0]] = product_nt(wt[:WIDE, :], xs[PARTS[0], :])
    tangent[...] = product_nt(wt[WIDE:, :], xs[PARTS[0], :])
    pre[:, PARTS[1]] = product_nt(wt[:WIDE, :], xs[PARTS[1], :])
    for index, rows in enumerate(ROWS):
        for part, lanes in enumerate(PARTS):
            slope, bend = gelu_slopes(pre[rows, lanes])
            upstream = upstream_rows(ups, number, index, lanes)
            first[rows, lanes] = (upstream * slope).astype(BF16)
            if part == 0:
                second[rows, :] = (upstream * (bend * tangent[rows, :])).astype(BF16)
    for half, lanes, tile in halves(core):
        total = grad[:, tile] + product(first[...], xs[:, tile])
        if half == 0:
            keep[:, lanes] = total
        else:
            give[:, lanes] = total.astype(BF16)


def last_gradient(number, place, blocks, weights, ups, grad):
    operands = (place, *blocks, *weights, *ups, grad)
    return pl.pallas_call(
        functools.partial(last_gradient_kernel, number),
        out_shape=(
            shape((WIDE, HALF), F32),
            shape((WIDE, HALF), BF16),
            shape((WIDE, 2 * TOK), BF16),
        ),
        in_specs=[spec(SMEM)] + [spec(ANY)] * 10 + [spec(VMEM)] * 6,
        out_specs=(spec(VMEM),) * 3,
        scratch_shapes=[
            VMEM((GROUP, D), BF16),
            VMEM((2 * WIDE, D), BF16),
            VMEM((WIDE, GROUP), F32),
            VMEM((WIDE, 2 * TOK), F32),
            VMEM((WIDE, GROUP), BF16),
            pltpu.SemaphoreType.DMA((2,)),
        ],
        compiler_params=params(24),
        cost_estimate=cost(5 << 29, 12 << 20, 1 << 19),
        name="last_gradient",
    )(*operands)


def last_hessian_kernel(place, b0, b1, b2, b3, second, hess, keep, give, xs, sems):
    tokens = [
        pltpu.make_async_copy(block.at[pl.ds(0, HESS), :], xs.at[pl.ds(index * HESS, HESS), :], sems.at[0])
        for index, block in enumerate((b0, b1, b2, b3))
    ]
    start(tokens)
    wait(tokens)
    for half, lanes, tile in halves(place[0]):
        total = hess[:, tile] + product(second[...], xs[:, tile])
        if half == 0:
            keep[:, lanes] = total
        else:
            give[:, lanes] = total.astype(BF16)


def last_hessian(place, blocks, second, hess):
    return pl.pallas_call(
        last_hessian_kernel,
        out_shape=(shape((WIDE, HALF), F32), shape((WIDE, HALF), BF16)),
        in_specs=[spec(SMEM)] + [spec(ANY)] * 4 + [spec(VMEM)] * 2,
        out_specs=(spec(VMEM),) * 2,
        scratch_shapes=[VMEM((2 * TOK, D), BF16), pltpu.SemaphoreType.DMA((1,))],
        compiler_params=params(12),
        cost_estimate=cost(1 << 29, 8 << 20),
        name="last_hessian",
    )(place, *blocks, second, hess)


def sophia_kernel(place, grad_mine, grad_theirs, hess_mine, hess_theirs, bits, moment, curvature, s0, s1, s2, s3, *refs):
    outs, stage, sems = refs[:3], refs[3:6], refs[6]
    core = place[0]
    squares = jnp.sum((s0[...] + s1[...]) + (s2[...] + s3[...]))
    scale = jnp.minimum(1.0, lax.rsqrt(squares / (D * FF) + 1e-06))
    copies = []
    for half, grad, hess in ((core, grad_mine, hess_mine), (1 - core, grad_theirs, hess_theirs)):
        for part in range(4):
            lanes = slice(part * 256, (part + 1) * 256)
            rows = pl.ds(pl.multiple_of(half * HALF + part * 256, 256), 256)
            probe = (2 * bits[rows, :] - 1).astype(F32)
            estimate = 2.0 * scale * probe * hess[:, lanes].T
            moment_out = beta_first * moment[rows, :] + (1.0 - beta_first) * scale * grad[:, lanes].T
            curvature_out = beta_second * curvature[rows, :] + (1.0 - beta_second) * estimate
            stage[0][rows, :] = moment_out
            stage[1][rows, :] = curvature_out
            stage[2][rows, :] = jnp.clip(
                moment_out / jnp.maximum(gamma_scale * curvature_out, floor_value), -1.0, 1.0
            )
            for index in range(3):
                copy = pltpu.make_async_copy(stage[index].at[rows, :], outs[index].at[rows, :], sems.at[index])
                copy.start()
                copies.append(copy)
    wait(copies)


def sophia_step(place, sums, state, squares):
    return pl.pallas_call(
        sophia_kernel,
        out_shape=(shape((D, HID), F32),) * 3,
        in_specs=[spec(SMEM)] + [spec(VMEM)] * 11,
        out_specs=(spec(ANY),) * 3,
        scratch_shapes=[VMEM((D, HID), F32)] * 3 + [pltpu.SemaphoreType.DMA((3,))],
        compiler_params=params(14),
        cost_estimate=cost(1 << 23, 8 << 20),
        name="sophia_step",
    )(place, *sums, *state, *squares)


def four(value, axes, pairs):
    return [value] + [lax.ppermute(value, axes, pair) for pair in pairs]


YL_Z = (
    ("yl", "z"),
    [
        [(y * 8 + z, (y ^ dy) * 8 + (z ^ dz)) for y in range(2) for z in range(8)]
        for dy, dz in ((1, 0), (0, 1), (1, 1))
    ],
)
Z = ("z", [[(z, (z + by) % 8) for z in range(8)] for by in (2, 6, 4)])
X = ("x", [[(x, (x + by) % 4) for x in range(4)] for by in (1, 3, 2)])


def local(tokens, cotangent, weight, probe_bits, moment, curvature):
    place = jnp.stack([lax.axis_index(axis) for axis in ("c", "x", "z", "yl")]).astype(jnp.int32)
    core = lax.axis_index("c")

    got = {(0, 0): tokens}
    got[0, -1] = shift(tokens, "z", 1)
    got[0, 1] = shift(tokens, "z", -1)
    got[1, 0] = shift(tokens, "yl", 1)
    own, sent = pack_weights(place, weight, probe_bits)
    right, left = shift(sent, "x", 1), shift(sent, "x", -1)

    place, (got[0, -1], got[0, 1], got[1, 0]) = after(place, (got[0, -1], got[0, 1], got[1, 0]))
    got[0, -2] = shift(got[0, -1], "z", 1)
    got[0, 2] = shift(got[0, 1], "z", -1)
    got[1, -1] = shift(got[0, -1], "yl", 1)
    mine = [right, left, shift(right[:HID], "x", 1), shift(left[HID:], "x", -1)]
    turned = pack_cotangent(place, cotangent)

    (mine, turned), (got[0, -2], got[0, 2], got[1, -1]) = after((mine, turned), (got[0, -2], got[0, 2], got[1, -1]))
    got[0, -3] = shift(got[0, -2], "z", 1)
    got[0, 3] = shift(got[0, 2], "z", -1)
    got[1, -2] = shift(got[0, -2], "yl", 1)
    theirs, turned = after(shift(join(mine), "c", 1), turned)
    right, left = shift(turned[1], "x", 1), shift(turned[2], "x", -1)
    weights = (own, *mine, theirs)
    factors = [*slopes(place, [got[key] for key in CHUNKS[0]], weights)]

    factors, (got[0, -3], got[0, 3], got[1, -2]) = after(factors, (got[0, -3], got[0, 3], got[1, -2]))
    got[0, -4] = shift(got[0, -3], "z", 1)
    got[1, 1] = shift(got[1, 0], "z", -1)
    got[1, -3] = shift(got[0, -3], "yl", 1)
    ups = [turned[0], right, left, shift(right[HID:], "x", 1), shift(left[HID:], "x", -1)]
    factors += slopes(place, [got[key] for key in CHUNKS[1]], weights)

    factors, (got[0, -4], got[1, 1], got[1, -3]) = after(factors, (got[0, -4], got[1, 1], got[1, -3]))
    got[1, -4] = shift(got[1, -3], "z", 1)
    got[1, 2] = shift(got[1, 1], "z", -1)
    got[1, 3] = shift(got[0, 3], "yl", 1)
    factors += slopes(place, [got[key] for key in CHUNKS[2]], weights)
    grad, hess = products([got[key] for chunk in CHUNKS[:3] for key in chunk], ups, factors)

    (grad, hess), (got[1, -4], got[1, 2], got[1, 3]) = after((grad, hess), (got[1, -4], got[1, 2], got[1, 3]))
    blocks = [got[key] for key in CHUNKS[3]]
    keep_grad, give_grad, second = last_gradient(3, place, blocks, weights, ups, grad)
    keep_hess, give_hess = last_hessian(place, blocks, second, hess)

    def over_cores(keep, give):
        keep = keep + shift(give, "c", 1).astype(F32)
        return keep[:HID], [keep[n * HID : (n + 1) * HID].astype(BF16) for n in range(1, 4)]

    def add_x(total, parts):
        for part in parts:
            total = total + part.astype(F32)
        return total.astype(BF16)

    def over_y(total):
        return total.astype(F32) + shift(total, "yh", 1).astype(F32)

    def over_x(own, sent):
        return add_x(own, [shift(part, "x", -hop) for hop, part in zip(HOPS[1:], sent)])

    gradient = over_y(over_x(*over_cores(keep_grad, give_grad)))
    hessian_vector = over_x(*over_cores(keep_hess, give_hess))
    gradient, hessian_vector = after(gradient, hessian_vector)
    gradients = (gradient, shift(gradient, "c", 1))
    squares = [jnp.sum((half * half).reshape(-1, 8, HALF // TOK, TOK), axis=(0, 2)) for half in gradients]
    squares, hessian_vector = after(sum(four(squares[0] + squares[1], *YL_Z)), over_y(hessian_vector))
    squares, other = after(sum(four(squares, *Z)), shift(hessian_vector, "c", 1))
    return sophia_step(
        place,
        (*gradients, hessian_vector, other),
        (probe_bits, moment, curvature),
        four(squares, *X),
    )


def solution(mesh):
    fine = Mesh(mesh.devices.reshape(tuple(SIZES.values())), AXES)
    dp, fsdp = ("yh", "c"), ("yl", "z", "x")
    return jax.shard_map(
        local,
        mesh=fine,
        in_specs=(
            P(dp + fsdp, None),
            P(dp, fsdp),
            P(None, fsdp),
            P(None, fsdp),
            P(None, fsdp),
            P(None, fsdp),
        ),
        out_specs=(P(None, fsdp), P(None, fsdp), P(None, fsdp)),
        check_vma=False,
    )
```

```python
import functools

import jax
import jax.numpy as jnp
from jax import lax
from jax.experimental import pallas as pl
from jax.experimental.pallas import tpu as pltpu
from jax.sharding import Mesh, PartitionSpec as P

D = 2048
FF = 8192
HALF = D // 2
TOK = 128
HESS = 64
HID = 128
WIDE = 4 * HID
GROUP = 4 * TOK

inv_root_two = 0.7071067811865476
inv_root_tau = 0.3989422804014327
beta_first = 0.96
beta_second = 0.99
gamma_scale = 0.5
floor_value = 0.1

SIZES = {"yl": 2, "z": 8, "x": 4, "yh": 2, "c": 2}
AXES = tuple(SIZES)
HOPS = (0, 1, -1, 2)
CHUNKS = (
    ((0, 0), (0, -1), (0, 1), (1, 0)),
    ((0, -2), (0, 2), (1, -1), (0, -3)),
    ((0, 3), (1, -2), (0, -4), (1, 1)),
    ((1, -3), (1, -4), (1, 2), (1, 3)),
)

F32, BF16 = jnp.float32, jnp.bfloat16
VMEM, SMEM, ANY = pltpu.VMEM, pltpu.SMEM, pl.ANY


def gelu_slopes(values):
    density = jnp.exp(-0.5 * values * values) * inv_root_tau
    normal_cdf = 0.5 * (1.0 + lax.erf(values * inv_root_two))
    return (normal_cdf + values * density, density * (2.0 - values * values))


def shape(dims, dtype):
    return jax.ShapeDtypeStruct(dims, dtype)


def spec(space):
    return pl.BlockSpec(memory_space=space)


def params(mib):
    return pltpu.CompilerParams(vmem_limit_bytes=mib << 20)


def cost(flops, moved, transcendentals=0):
    return pl.CostEstimate(flops=flops, bytes_accessed=moved, transcendentals=transcendentals)


def shift(value, axis, by):
    n = SIZES[axis]
    with jax.named_scope("%s%d" % (axis, by)):
        return lax.ppermute(value, axis, [(i, (i + by) % n) for i in range(n)])


def after(values, done):
    return lax.optimization_barrier((values, done))


def weights_kernel(place, weight, bits, own, mine, weight_in, bits_in, sems):
    parts = 4
    copies = []
    for part in range(parts):
        rows = pl.ds(part * (D // parts), D // parts)
        copies.append(
            [
                pltpu.make_async_copy(weight.at[rows, :], weight_in.at[rows, :], sems.at[part]),
                pltpu.make_async_copy(bits.at[rows, :], bits_in.at[rows, :], sems.at[part]),
            ]
        )
        for copy in copies[-1]:
            copy.start()
    for part in range(parts):
        for copy in copies[part]:
            copy.wait()
        rows = slice(part * (D // parts), (part + 1) * (D // parts))
        own[:HID, rows] = weight_in[rows, :].T.astype(BF16)
        own[HID:, rows] = (2 * bits_in[rows, :] - 1).astype(F32).T.astype(BF16)
    mine[...] = own[:, pl.ds(pl.multiple_of(place[0] * HALF, HALF), HALF)]


def pack_weights(place, weight, bits):
    return pl.pallas_call(
        weights_kernel,
        out_shape=(shape((2 * HID, D), BF16), shape((2 * HID, HALF), BF16)),
        in_specs=[spec(SMEM), spec(ANY), spec(ANY)],
        out_specs=(spec(VMEM), spec(VMEM)),
        scratch_shapes=[VMEM((D, HID), F32), VMEM((D, HID), jnp.int32), pltpu.SemaphoreType.DMA((4,))],
        compiler_params=params(8),
        cost_estimate=cost(1 << 20, 4 << 20),
        name="pack_weights",
    )(place, weight, bits)


def join_kernel(first, second, third, fourth, out, sems):
    copies = []
    row = 0
    for index, part in enumerate((first, second, third, fourth)):
        rows = part.shape[0]
        copies.append(pltpu.make_async_copy(part, out.at[pl.ds(row, rows), :], sems.at[index]))
        row += rows
    for copy in copies:
        copy.start()
    for copy in copies:
        copy.wait()


def join(parts):
    return pl.pallas_call(
        join_kernel,
        out_shape=shape((6 * HID, HALF), BF16),
        in_specs=[spec(ANY)] * 4,
        out_specs=spec(ANY),
        scratch_shapes=[pltpu.SemaphoreType.DMA((4,))],
        compiler_params=params(4),
        cost_estimate=cost(0, 3 << 20),
        name="join",
    )(*parts)


def cotangent_kernel(place, cotangent, own, right, left):
    x, z, yl = place[1], place[2], place[3]
    for hop in HOPS:
        for number, chunk in enumerate(CHUNKS):
            starts = []
            for other, dz in chunk:
                row = lax.rem(yl + other, 2) * 8 + lax.rem(z + (dz + 8), 8)
                starts.append((row * 4 + lax.rem(x + (hop + 4), 4)) * TOK)
            for part in range(2):
                for pair in range(2):
                    rows = [
                        cotangent[pl.ds(pl.multiple_of(start + part * HESS, HESS), HESS), :]
                        for start in starts[2 * pair : 2 * pair + 2]
                    ]
                    turned = jnp.concatenate(rows, axis=0).T
                    lane = number * GROUP + part * 2 * TOK + pair * TOK
                    lanes = slice(lane, lane + TOK)
                    if hop == 2:
                        right[HID:, lanes] = turned[: HID // 2]
                        left[HID:, lanes] = turned[HID // 2 :]
                    else:
                        out = {0: own, 1: right, -1: left}[hop]
                        out[:HID, lanes] = turned


def pack_cotangent(place, cotangent):
    sent = shape((HID + HID // 2, 4 * GROUP), BF16)
    return pl.pallas_call(
        cotangent_kernel,
        out_shape=(shape((HID, 4 * GROUP), BF16), sent, sent),
        in_specs=[spec(SMEM), spec(VMEM)],
        out_specs=(spec(VMEM),) * 3,
        compiler_params=params(10),
        cost_estimate=cost(1 << 20, 4 << 20),
        name="pack_cotangent",
    )(place, cotangent)


def product(left, right):
    return lax.dot_general(left, right, (((1,), (0,)), ((), ())), preferred_element_type=F32)


def product_nt(left, right):
    return lax.dot_general(left, right, (((1,), (1,)), ((), ())), preferred_element_type=F32)


def token_copies(blocks, xs, base, sem):
    return [
        pltpu.make_async_copy(
            block.at[pl.ds(part * HESS, HESS), :],
            xs.at[pl.ds(base + part * 2 * TOK + index * HESS, HESS), :],
            sem,
        )
        for index, block in enumerate(blocks)
        for part in range(2)
    ]


def weight_copies(core, own, mine, theirs, wt, sem):
    copies = []
    for kind in range(2):
        copies.append(pltpu.make_async_copy(own.at[pl.ds(kind * HID, HID), :], wt.at[pl.ds(kind * WIDE, HID), :], sem))
        for index in range(3):
            start_row = index * 2 * HID + kind * HID
            rows = pl.ds(kind * WIDE + (index + 1) * HID, HID)
            source = mine[index].at[pl.ds(kind * HID, HID), :] if index < 2 else mine[2 + kind]
            lanes = pl.ds(pl.multiple_of(core * HALF, HALF), HALF)
            copies.append(pltpu.make_async_copy(source, wt.at[rows, lanes], sem))
            lanes = pl.ds(pl.multiple_of((1 - core) * HALF, HALF), HALF)
            copies.append(pltpu.make_async_copy(theirs.at[pl.ds(start_row, HID), :], wt.at[rows, lanes], sem))
    return copies


def upstream_rows(ups, number, index, lanes):
    own, right, left, low, high = ups
    source, row = ((own, 0), (own, 64), (right, 0), (right, 64), (left, 0), (left, 64), (low, 0), (high, 0))[index]
    return source[row : row + 64, number * GROUP + lanes.start : number * GROUP + lanes.stop].astype(F32)


def start(copies):
    for copy in copies:
        copy.start()


def wait(copies):
    for copy in copies:
        copy.wait()


ROWS = [slice(row, row + 64) for row in range(0, WIDE, 64)]
PARTS = [slice(0, 2 * TOK), slice(2 * TOK, GROUP)]


def slopes_of(xs, wt, slope, curve, pre, tangent):
    pre[:, PARTS[0]] = product_nt(wt[:WIDE, :], xs[PARTS[0], :])
    tangent[...] = product_nt(wt[WIDE:, :], xs[PARTS[0], :])
    pre[:, PARTS[1]] = product_nt(wt[:WIDE, :], xs[PARTS[1], :])
    for rows in ROWS:
        for part, lanes in enumerate(PARTS):
            one, two = gelu_slopes(pre[rows, lanes])
            slope[rows, lanes] = one
            if part == 0:
                curve[rows, :] = two * tangent[rows, :]


def first_slopes_kernel(place, b0, b1, b2, b3, own, m0, m1, m2, m3, theirs, slope, curve, wt, xs, pre, tangent, sems):
    tokens = token_copies((b0, b1, b2, b3), xs, 0, sems.at[0])
    weights = weight_copies(place[0], own, (m0, m1, m2, m3), theirs, wt, sems.at[1])
    start(tokens)
    start(weights)
    wait(tokens)
    wait(weights)
    slopes_of(xs, wt, slope, curve, pre, tangent)


def slopes_kernel(b0, b1, b2, b3, wt, slope, curve, xs, pre, tangent, sems):
    tokens = token_copies((b0, b1, b2, b3), xs, 0, sems.at[0])
    start(tokens)
    wait(tokens)
    slopes_of(xs, wt, slope, curve, pre, tangent)


SLOPES = (shape((WIDE, GROUP), F32), shape((WIDE, 2 * TOK), F32))
SLOPES_SCRATCH = (
    VMEM((GROUP, D), BF16),
    VMEM((WIDE, GROUP), F32),
    VMEM((WIDE, 2 * TOK), F32),
    pltpu.SemaphoreType.DMA((2,)),
)


def first_slopes(place, blocks, weights):
    *factors, wt = pl.pallas_call(
        first_slopes_kernel,
        out_shape=SLOPES + (shape((2 * WIDE, D), BF16),),
        in_specs=[spec(SMEM)] + [spec(ANY)] * 10,
        out_specs=(spec(VMEM),) * 3,
        scratch_shapes=SLOPES_SCRATCH,
        compiler_params=params(14),
        cost_estimate=cost(3 << 29, 8 << 20, 1 << 19),
        name="first_slopes",
    )(place, *blocks, *weights)
    return factors, wt


def slopes(blocks, wt):
    return pl.pallas_call(
        slopes_kernel,
        out_shape=SLOPES,
        in_specs=[spec(ANY)] * 4 + [spec(VMEM)],
        out_specs=(spec(VMEM),) * 2,
        scratch_shapes=SLOPES_SCRATCH,
        compiler_params=params(14),
        cost_estimate=cost(3 << 29, 8 << 20, 1 << 19),
        name="slopes",
    )(*blocks, wt)


def products_kernel(chunks, *refs):
    blocks, ups = refs[: 4 * chunks], refs[4 * chunks : 4 * chunks + 5]
    factors = refs[4 * chunks + 5 : 6 * chunks + 5]
    grad, hess, xs, first, second, sems = refs[6 * chunks + 5 :]
    tokens = []
    for number in range(chunks):
        tokens += token_copies(blocks[4 * number : 4 * number + 4], xs, number * GROUP, sems.at[0])
    start(tokens)
    for number in range(chunks):
        slope, curve = factors[2 * number : 2 * number + 2]
        for index, rows in enumerate(ROWS):
            for part, lanes in enumerate(PARTS):
                upstream = upstream_rows(ups, number, index, lanes)
                first[rows, number * GROUP + lanes.start : number * GROUP + lanes.stop] = (
                    upstream * slope[rows, lanes]
                ).astype(BF16)
                if part == 0:
                    second[rows, number * 2 * TOK : (number + 1) * 2 * TOK] = (upstream * curve[rows, :]).astype(BF16)
    wait(tokens)
    for column in range(0, D, 256):
        lanes = slice(column, column + 256)
        grad[:, lanes] = product(first[...], xs[:, lanes])
        part = product(second[:, : 2 * TOK], xs[: 2 * TOK, lanes])
        for number in range(1, chunks):
            part += product(
                second[:, number * 2 * TOK : (number + 1) * 2 * TOK],
                xs[number * GROUP : number * GROUP + 2 * TOK, lanes],
            )
        hess[:, lanes] = part


def products(blocks, ups, factors):
    chunks = len(factors) // 2
    operands = (*blocks, *ups, *factors)
    return pl.pallas_call(
        functools.partial(products_kernel, chunks),
        out_shape=(shape((WIDE, D), F32),) * 2,
        in_specs=[spec(ANY)] * len(blocks) + [spec(VMEM)] * (len(operands) - len(blocks)),
        out_specs=(spec(VMEM),) * 2,
        scratch_shapes=[
            VMEM((chunks * GROUP, D), BF16),
            VMEM((WIDE, chunks * GROUP), BF16),
            VMEM((WIDE, chunks * 2 * TOK), BF16),
            pltpu.SemaphoreType.DMA((1,)),
        ],
        compiler_params=params(30),
        cost_estimate=cost(5 << 30, 24 << 20),
        name="products",
    )(*operands)


def half_tiles(half):
    return [
        (slice(column, column + 256), pl.ds(pl.multiple_of(half * HALF + column, 256), 256))
        for column in range(0, HALF, 256)
    ]


def last_slopes_kernel(number, *refs):
    place, blocks, wt, ups, grad = refs[0], refs[1:5], refs[5], refs[6:11], refs[11]
    give, first, second, xs, pre, tangent, sems = refs[12:]
    tokens = token_copies(blocks, xs, 0, sems.at[0])
    start(tokens)
    wait(tokens)
    pre[:, PARTS[0]] = product_nt(wt[:WIDE, :], xs[PARTS[0], :])
    tangent[...] = product_nt(wt[WIDE:, :], xs[PARTS[0], :])
    pre[:, PARTS[1]] = product_nt(wt[:WIDE, :], xs[PARTS[1], :])
    for index, rows in enumerate(ROWS):
        for part, lanes in enumerate(PARTS):
            slope, bend = gelu_slopes(pre[rows, lanes])
            upstream = upstream_rows(ups, number, index, lanes)
            first[rows, lanes] = (upstream * slope).astype(BF16)
            if part == 0:
                second[rows, :] = (upstream * (bend * tangent[rows, :])).astype(BF16)
    for lanes, tile in half_tiles(1 - place[0]):
        give[:, lanes] = (grad[:, tile] + product(first[...], xs[:, tile])).astype(BF16)


def last_slopes(number, place, blocks, wt, ups, grad):
    operands = (place, *blocks, wt, *ups, grad)
    return pl.pallas_call(
        functools.partial(last_slopes_kernel, number),
        out_shape=(
            shape((WIDE, HALF), BF16),
            shape((WIDE, GROUP), BF16),
            shape((WIDE, 2 * TOK), BF16),
            shape((GROUP, D), BF16),
        ),
        in_specs=[spec(SMEM)] + [spec(ANY)] * 4 + [spec(VMEM)] * 7,
        out_specs=(spec(VMEM),) * 4,
        scratch_shapes=[
            VMEM((WIDE, GROUP), F32),
            VMEM((WIDE, 2 * TOK), F32),
            pltpu.SemaphoreType.DMA((1,)),
        ],
        compiler_params=params(26),
        cost_estimate=cost(5 << 29, 12 << 20, 1 << 19),
        name="last_slopes",
    )(*operands)


def last_halves_kernel(place, first, second, xs, grad, hess, keep_grad, keep_hess, give_hess):
    core = place[0]
    for lanes, tile in half_tiles(1 - core):
        give_hess[:, lanes] = (hess[:, tile] + product(second[...], xs[PARTS[0], tile])).astype(BF16)
    for lanes, tile in half_tiles(core):
        keep_hess[:, lanes] = hess[:, tile] + product(second[...], xs[PARTS[0], tile])
        keep_grad[:, lanes] = grad[:, tile] + product(first[...], xs[:, tile])


def last_halves(place, *operands):
    return pl.pallas_call(
        last_halves_kernel,
        out_shape=(shape((WIDE, HALF), F32), shape((WIDE, HALF), F32), shape((WIDE, HALF), BF16)),
        in_specs=[spec(SMEM)] + [spec(VMEM)] * 5,
        out_specs=(spec(VMEM),) * 3,
        compiler_params=params(22),
        cost_estimate=cost(1 << 30, 12 << 20),
        name="last_halves",
    )(place, *operands)


def sophia_kernel(place, grad_mine, grad_theirs, hess_mine, hess_theirs, bits, moment, curvature, s0, s1, s2, s3, *refs):
    outs, stage, sems = refs[:3], refs[3:6], refs[6]
    core = place[0]
    squares = jnp.sum((s0[...] + s1[...]) + (s2[...] + s3[...]))
    scale = jnp.minimum(1.0, lax.rsqrt(squares / (D * FF) + 1e-06))
    copies = []
    for half, grad, hess in ((core, grad_mine, hess_mine), (1 - core, grad_theirs, hess_theirs)):
        for part in range(4):
            lanes = slice(part * 256, (part + 1) * 256)
            rows = pl.ds(pl.multiple_of(half * HALF + part * 256, 256), 256)
            probe = (2 * bits[rows, :] - 1).astype(F32)
            estimate = 2.0 * scale * probe * hess[:, lanes].T
            moment_out = beta_first * moment[rows, :] + (1.0 - beta_first) * scale * grad[:, lanes].T
            curvature_out = beta_second * curvature[rows, :] + (1.0 - beta_second) * estimate
            stage[0][rows, :] = moment_out
            stage[1][rows, :] = curvature_out
            stage[2][rows, :] = jnp.clip(
                moment_out / jnp.maximum(gamma_scale * curvature_out, floor_value), -1.0, 1.0
            )
            for index in range(3):
                copy = pltpu.make_async_copy(stage[index].at[rows, :], outs[index].at[rows, :], sems.at[index])
                copy.start()
                copies.append(copy)
    wait(copies)


def sophia_step(place, sums, state, squares):
    return pl.pallas_call(
        sophia_kernel,
        out_shape=(shape((D, HID), F32),) * 3,
        in_specs=[spec(SMEM)] + [spec(VMEM)] * 11,
        out_specs=(spec(ANY),) * 3,
        scratch_shapes=[VMEM((D, HID), F32)] * 3 + [pltpu.SemaphoreType.DMA((3,))],
        compiler_params=params(14),
        cost_estimate=cost(1 << 23, 8 << 20),
        name="sophia_step",
    )(place, *sums, *state, *squares)


def four(value, axes, pairs):
    return [value] + [lax.ppermute(value, axes, pair) for pair in pairs]


YL_Z = (
    ("yl", "z"),
    [
        [(y * 8 + z, (y ^ dy) * 8 + (z ^ dz)) for y in range(2) for z in range(8)]
        for dy, dz in ((1, 0), (0, 1), (1, 1))
    ],
)
Z = ("z", [[(z, (z + by) % 8) for z in range(8)] for by in (2, 6, 4)])
X = ("x", [[(x, (x + by) % 4) for x in range(4)] for by in (1, 3, 2)])


def local(tokens, cotangent, weight, probe_bits, moment, curvature):
    place = jnp.stack([lax.axis_index(axis) for axis in ("c", "x", "z", "yl")]).astype(jnp.int32)
    core = lax.axis_index("c")

    got = {(0, 0): tokens}
    got[0, -1] = shift(tokens, "z", 1)
    got[0, 1] = shift(tokens, "z", -1)
    got[1, 0] = shift(tokens, "yl", 1)
    own, sent = pack_weights(place, weight, probe_bits)
    right, left = shift(sent, "x", 1), shift(sent, "x", -1)

    place, (got[0, -1], got[0, 1], got[1, 0]) = after(place, (got[0, -1], got[0, 1], got[1, 0]))
    got[0, -2] = shift(got[0, -1], "z", 1)
    got[0, 2] = shift(got[0, 1], "z", -1)
    got[1, -1] = shift(got[0, -1], "yl", 1)
    mine = [right, left, shift(right[:HID], "x", 1), shift(left[HID:], "x", -1)]
    turned = pack_cotangent(place, cotangent)

    (mine, turned), (got[0, -2], got[0, 2], got[1, -1]) = after((mine, turned), (got[0, -2], got[0, 2], got[1, -1]))
    got[0, -3] = shift(got[0, -2], "z", 1)
    got[0, 3] = shift(got[0, 2], "z", -1)
    got[1, -2] = shift(got[0, -2], "yl", 1)
    theirs, turned = after(shift(join(mine), "c", 1), turned)
    right, left = shift(turned[1], "x", 1), shift(turned[2], "x", -1)
    factors, wt = first_slopes(place, [got[key] for key in CHUNKS[0]], (own, *mine, theirs))

    factors, (got[0, -3], got[0, 3], got[1, -2]) = after(factors, (got[0, -3], got[0, 3], got[1, -2]))
    got[0, -4] = shift(got[0, -3], "z", 1)
    got[1, 1] = shift(got[1, 0], "z", -1)
    got[1, -3] = shift(got[0, -3], "yl", 1)
    ups = [turned[0], right, left, shift(right[HID:], "x", 1), shift(left[HID:], "x", -1)]
    factors += slopes([got[key] for key in CHUNKS[1]], wt)

    factors, (got[0, -4], got[1, 1], got[1, -3]) = after(factors, (got[0, -4], got[1, 1], got[1, -3]))
    got[1, -4] = shift(got[1, -3], "z", 1)
    got[1, 2] = shift(got[1, 1], "z", -1)
    got[1, 3] = shift(got[0, 3], "yl", 1)
    factors += slopes([got[key] for key in CHUNKS[2]], wt)
    grad, hess = products([got[key] for chunk in CHUNKS[:3] for key in chunk], ups, factors)

    (grad, hess), (got[1, -4], got[1, 2], got[1, 3]) = after((grad, hess), (got[1, -4], got[1, 2], got[1, 3]))
    blocks = [got[key] for key in CHUNKS[3]]
    give_grad, first, second, last_tokens = last_slopes(3, place, blocks, wt, ups, grad)
    keep_grad, keep_hess, give_hess = last_halves(place, first, second, last_tokens, grad, hess)

    def over_cores(keep, give):
        keep = keep + shift(give, "c", 1).astype(F32)
        return keep[:HID], [keep[n * HID : (n + 1) * HID].astype(BF16) for n in range(1, 4)]

    def add_x(total, parts):
        for part in parts:
            total = total + part.astype(F32)
        return total.astype(BF16)

    def over_y(total):
        return total.astype(F32) + shift(total, "yh", 1).astype(F32)

    def over_x(own, sent):
        return add_x(own, [shift(part, "x", -hop) for hop, part in zip(HOPS[1:], sent)])

    gradient = over_y(over_x(*over_cores(keep_grad, give_grad)))
    hessian_vector = over_x(*over_cores(keep_hess, give_hess))
    gradient, hessian_vector = after(gradient, hessian_vector)
    gradients = (gradient, shift(gradient, "c", 1))
    squares = [jnp.sum((half * half).reshape(-1, 8, HALF // TOK, TOK), axis=(0, 2)) for half in gradients]
    squares, hessian_vector = after(sum(four(squares[0] + squares[1], *YL_Z)), over_y(hessian_vector))
    squares, other = after(sum(four(squares, *Z)), shift(hessian_vector, "c", 1))
    return sophia_step(
        place,
        (*gradients, hessian_vector, other),
        (probe_bits, moment, curvature),
        four(squares, *X),
    )


def solution(mesh):
    fine = Mesh(mesh.devices.reshape(tuple(SIZES.values())), AXES)
    dp, fsdp = ("yh", "c"), ("yl", "z", "x")
    return jax.shard_map(
        local,
        mesh=fine,
        in_specs=(
            P(dp + fsdp, None),
            P(dp, fsdp),
            P(None, fsdp),
            P(None, fsdp),
            P(None, fsdp),
            P(None, fsdp),
        ),
        out_specs=(P(None, fsdp), P(None, fsdp), P(None, fsdp)),
        check_vma=False,
    )
```

```python
import functools

import jax
import jax.numpy as jnp
from jax import lax
from jax.experimental import pallas as pl
from jax.experimental.pallas import tpu as pltpu
from jax.sharding import Mesh, PartitionSpec as P

D = 2048
FF = 8192
HALF = D // 2
TOK = 128
HESS = 64
HID = 128
WIDE = 4 * HID
GROUP = 4 * TOK

inv_root_two = 0.7071067811865476
inv_root_tau = 0.3989422804014327
beta_first = 0.96
beta_second = 0.99
gamma_scale = 0.5
floor_value = 0.1

SIZES = {"yl": 2, "z": 8, "x": 4, "yh": 2, "c": 2}
AXES = tuple(SIZES)
HOPS = (0, 1, -1, 2)
CHUNKS = (
    ((0, 0), (0, -1), (0, 1), (1, 0)),
    ((0, -2), (0, 2), (1, -1), (0, -3)),
    ((0, 3), (1, -2), (0, -4), (1, 1)),
    ((1, -3), (1, 3), (1, -4), (1, 2)),
)

F32, BF16 = jnp.float32, jnp.bfloat16
VMEM, SMEM, ANY = pltpu.VMEM, pltpu.SMEM, pl.ANY


def gelu_slopes(values):
    density = jnp.exp(-0.5 * values * values) * inv_root_tau
    normal_cdf = 0.5 * (1.0 + lax.erf(values * inv_root_two))
    return (normal_cdf + values * density, density * (2.0 - values * values))


def shape(dims, dtype):
    return jax.ShapeDtypeStruct(dims, dtype)


def spec(space):
    return pl.BlockSpec(memory_space=space)


def params(mib):
    return pltpu.CompilerParams(vmem_limit_bytes=mib << 20)


def cost(flops, moved, transcendentals=0):
    return pl.CostEstimate(flops=flops, bytes_accessed=moved, transcendentals=transcendentals)


def shift(value, axis, by):
    n = SIZES[axis]
    with jax.named_scope("%s%d" % (axis, by)):
        return lax.ppermute(value, axis, [(i, (i + by) % n) for i in range(n)])


def after(values, done):
    return lax.optimization_barrier((values, done))


def weights_kernel(place, weight, bits, own, mine, weight_in, bits_in, sems):
    parts = 4
    copies = []
    for part in range(parts):
        rows = pl.ds(part * (D // parts), D // parts)
        copies.append(
            [
                pltpu.make_async_copy(weight.at[rows, :], weight_in.at[rows, :], sems.at[part]),
                pltpu.make_async_copy(bits.at[rows, :], bits_in.at[rows, :], sems.at[part]),
            ]
        )
        for copy in copies[-1]:
            copy.start()
    for part in range(parts):
        for copy in copies[part]:
            copy.wait()
        rows = slice(part * (D // parts), (part + 1) * (D // parts))
        own[:HID, rows] = weight_in[rows, :].T.astype(BF16)
        own[HID:, rows] = (2 * bits_in[rows, :] - 1).astype(F32).T.astype(BF16)
    mine[...] = own[:, pl.ds(pl.multiple_of(place[0] * HALF, HALF), HALF)]


def pack_weights(place, weight, bits):
    return pl.pallas_call(
        weights_kernel,
        out_shape=(shape((2 * HID, D), BF16), shape((2 * HID, HALF), BF16)),
        in_specs=[spec(SMEM), spec(ANY), spec(ANY)],
        out_specs=(spec(VMEM), spec(VMEM)),
        scratch_shapes=[VMEM((D, HID), F32), VMEM((D, HID), jnp.int32), pltpu.SemaphoreType.DMA((4,))],
        compiler_params=params(8),
        cost_estimate=cost(1 << 20, 4 << 20),
        name="pack_weights",
    )(place, weight, bits)


def join_kernel(first, second, third, fourth, out, sems):
    copies = []
    row = 0
    for index, part in enumerate((first, second, third, fourth)):
        rows = part.shape[0]
        copies.append(pltpu.make_async_copy(part, out.at[pl.ds(row, rows), :], sems.at[index]))
        row += rows
    for copy in copies:
        copy.start()
    for copy in copies:
        copy.wait()


def join(parts):
    return pl.pallas_call(
        join_kernel,
        out_shape=shape((6 * HID, HALF), BF16),
        in_specs=[spec(ANY)] * 4,
        out_specs=spec(ANY),
        scratch_shapes=[pltpu.SemaphoreType.DMA((4,))],
        compiler_params=params(4),
        cost_estimate=cost(0, 3 << 20),
        name="join",
    )(*parts)


def cotangent_kernel(place, cotangent, own, right, left):
    x, z, yl = place[1], place[2], place[3]
    for hop in HOPS:
        for number, chunk in enumerate(CHUNKS):
            starts = []
            for other, dz in chunk:
                row = lax.rem(yl + other, 2) * 8 + lax.rem(z + (dz + 8), 8)
                starts.append((row * 4 + lax.rem(x + (hop + 4), 4)) * TOK)
            for part in range(2):
                for pair in range(2):
                    rows = [
                        cotangent[pl.ds(pl.multiple_of(start + part * HESS, HESS), HESS), :]
                        for start in starts[2 * pair : 2 * pair + 2]
                    ]
                    turned = jnp.concatenate(rows, axis=0).T
                    lane = number * GROUP + part * 2 * TOK + pair * TOK
                    lanes = slice(lane, lane + TOK)
                    if hop == 2:
                        right[HID:, lanes] = turned[: HID // 2]
                        left[HID:, lanes] = turned[HID // 2 :]
                    else:
                        out = {0: own, 1: right, -1: left}[hop]
                        out[:HID, lanes] = turned


def pack_cotangent(place, cotangent):
    sent = shape((HID + HID // 2, 4 * GROUP), BF16)
    return pl.pallas_call(
        cotangent_kernel,
        out_shape=(shape((HID, 4 * GROUP), BF16), sent, sent),
        in_specs=[spec(SMEM), spec(VMEM)],
        out_specs=(spec(VMEM),) * 3,
        compiler_params=params(10),
        cost_estimate=cost(1 << 20, 4 << 20),
        name="pack_cotangent",
    )(place, cotangent)


def product(left, right):
    return lax.dot_general(left, right, (((1,), (0,)), ((), ())), preferred_element_type=F32)


def product_nt(left, right):
    return lax.dot_general(left, right, (((1,), (1,)), ((), ())), preferred_element_type=F32)


def token_copies(blocks, xs, base, sem):
    return [
        pltpu.make_async_copy(
            block.at[pl.ds(part * HESS, HESS), :],
            xs.at[pl.ds(base + part * 2 * TOK + index * HESS, HESS), :],
            sem,
        )
        for index, block in enumerate(blocks)
        for part in range(2)
    ]


def weight_copies(core, own, mine, theirs, wt, sem):
    copies = []
    for kind in range(2):
        copies.append(pltpu.make_async_copy(own.at[pl.ds(kind * HID, HID), :], wt.at[pl.ds(kind * WIDE, HID), :], sem))
        for index in range(3):
            start_row = index * 2 * HID + kind * HID
            rows = pl.ds(kind * WIDE + (index + 1) * HID, HID)
            source = mine[index].at[pl.ds(kind * HID, HID), :] if index < 2 else mine[2 + kind]
            lanes = pl.ds(pl.multiple_of(core * HALF, HALF), HALF)
            copies.append(pltpu.make_async_copy(source, wt.at[rows, lanes], sem))
            lanes = pl.ds(pl.multiple_of((1 - core) * HALF, HALF), HALF)
            copies.append(pltpu.make_async_copy(theirs.at[pl.ds(start_row, HID), :], wt.at[rows, lanes], sem))
    return copies


def upstream_rows(ups, number, index, lanes):
    own, right, left, low, high = ups
    source, row = ((own, 0), (own, 64), (right, 0), (right, 64), (left, 0), (left, 64), (low, 0), (high, 0))[index]
    return source[row : row + 64, number * GROUP + lanes.start : number * GROUP + lanes.stop].astype(F32)


def start(copies):
    for copy in copies:
        copy.start()


def wait(copies):
    for copy in copies:
        copy.wait()


ROWS = [slice(row, row + 64) for row in range(0, WIDE, 64)]
PARTS = [slice(0, 2 * TOK), slice(2 * TOK, GROUP)]


def slopes_of(xs, wt, slope, curve, pre, tangent):
    pre[:, PARTS[0]] = product_nt(wt[:WIDE, :], xs[PARTS[0], :])
    tangent[...] = product_nt(wt[WIDE:, :], xs[PARTS[0], :])
    pre[:, PARTS[1]] = product_nt(wt[:WIDE, :], xs[PARTS[1], :])
    for rows in ROWS:
        for part, lanes in enumerate(PARTS):
            one, two = gelu_slopes(pre[rows, lanes])
            slope[rows, lanes] = one
            if part == 0:
                curve[rows, :] = two * tangent[rows, :]


def first_slopes_kernel(place, b0, b1, b2, b3, own, m0, m1, m2, m3, theirs, slope, curve, wt, xs, pre, tangent, sems):
    tokens = token_copies((b0, b1, b2, b3), xs, 0, sems.at[0])
    weights = weight_copies(place[0], own, (m0, m1, m2, m3), theirs, wt, sems.at[1])
    start(tokens)
    start(weights)
    wait(tokens)
    wait(weights)
    slopes_of(xs, wt, slope, curve, pre, tangent)


def slopes_kernel(b0, b1, b2, b3, wt, slope, curve, xs, pre, tangent, sems):
    tokens = token_copies((b0, b1, b2, b3), xs, 0, sems.at[0])
    start(tokens)
    wait(tokens)
    slopes_of(xs, wt, slope, curve, pre, tangent)


SLOPES = (shape((WIDE, GROUP), F32), shape((WIDE, 2 * TOK), F32))
SLOPES_SCRATCH = (
    VMEM((GROUP, D), BF16),
    VMEM((WIDE, GROUP), F32),
    VMEM((WIDE, 2 * TOK), F32),
    pltpu.SemaphoreType.DMA((2,)),
)


def first_slopes(place, blocks, weights):
    *factors, wt = pl.pallas_call(
        first_slopes_kernel,
        out_shape=SLOPES + (shape((2 * WIDE, D), BF16),),
        in_specs=[spec(SMEM)] + [spec(ANY)] * 10,
        out_specs=(spec(VMEM),) * 3,
        scratch_shapes=SLOPES_SCRATCH,
        compiler_params=params(14),
        cost_estimate=cost(3 << 29, 8 << 20, 1 << 19),
        name="first_slopes",
    )(place, *blocks, *weights)
    return factors, wt


def slopes(blocks, wt):
    return pl.pallas_call(
        slopes_kernel,
        out_shape=SLOPES,
        in_specs=[spec(ANY)] * 4 + [spec(VMEM)],
        out_specs=(spec(VMEM),) * 2,
        scratch_shapes=SLOPES_SCRATCH,
        compiler_params=params(14),
        cost_estimate=cost(3 << 29, 8 << 20, 1 << 19),
        name="slopes",
    )(*blocks, wt)


def products_kernel(chunks, *refs):
    blocks, ups = refs[: 4 * chunks], refs[4 * chunks : 4 * chunks + 5]
    factors = refs[4 * chunks + 5 : 6 * chunks + 5]
    grad, hess, xs, first, second, sems = refs[6 * chunks + 5 :]
    tokens = []
    for number in range(chunks):
        tokens += token_copies(blocks[4 * number : 4 * number + 4], xs, number * GROUP, sems.at[0])
    start(tokens)
    for number in range(chunks):
        slope, curve = factors[2 * number : 2 * number + 2]
        for index, rows in enumerate(ROWS):
            for part, lanes in enumerate(PARTS):
                upstream = upstream_rows(ups, number, index, lanes)
                first[rows, number * GROUP + lanes.start : number * GROUP + lanes.stop] = (
                    upstream * slope[rows, lanes]
                ).astype(BF16)
                if part == 0:
                    second[rows, number * 2 * TOK : (number + 1) * 2 * TOK] = (upstream * curve[rows, :]).astype(BF16)
    wait(tokens)
    for column in range(0, D, 256):
        lanes = slice(column, column + 256)
        grad[:, lanes] = product(first[...], xs[:, lanes])
        part = product(second[:, : 2 * TOK], xs[: 2 * TOK, lanes])
        for number in range(1, chunks):
            part += product(
                second[:, number * 2 * TOK : (number + 1) * 2 * TOK],
                xs[number * GROUP : number * GROUP + 2 * TOK, lanes],
            )
        hess[:, lanes] = part


def products(blocks, ups, factors):
    chunks = len(factors) // 2
    operands = (*blocks, *ups, *factors)
    return pl.pallas_call(
        functools.partial(products_kernel, chunks),
        out_shape=(shape((WIDE, D), F32),) * 2,
        in_specs=[spec(ANY)] * len(blocks) + [spec(VMEM)] * (len(operands) - len(blocks)),
        out_specs=(spec(VMEM),) * 2,
        scratch_shapes=[
            VMEM((chunks * GROUP, D), BF16),
            VMEM((WIDE, chunks * GROUP), BF16),
            VMEM((WIDE, chunks * 2 * TOK), BF16),
            pltpu.SemaphoreType.DMA((1,)),
        ],
        compiler_params=params(30),
        cost_estimate=cost(5 << 30, 24 << 20),
        name="products",
    )(*operands)


def half_tiles(half):
    return [
        (slice(column, column + 256), pl.ds(pl.multiple_of(half * HALF + column, 256), 256))
        for column in range(0, HALF, 256)
    ]


def pair_terms(pair, blocks, wt, ups, first, second, xs, pre, tangent, sem):
    copies = [
        pltpu.make_async_copy(
            block.at[pl.ds(part * HESS, HESS), :], xs.at[pl.ds(part * TOK + index * HESS, HESS), :], sem
        )
        for index, block in enumerate(blocks)
        for part in range(2)
    ]
    start(copies)
    wait(copies)
    pre[...] = product_nt(wt[:WIDE, :], xs[...])
    tangent[...] = product_nt(wt[WIDE:, :], xs[:TOK, :])
    for index, rows in enumerate(ROWS):
        for part in range(2):
            lanes = slice(part * TOK, (part + 1) * TOK)
            lane = part * 2 * TOK + pair * TOK
            slope, bend = gelu_slopes(pre[rows, lanes])
            upstream = upstream_rows(ups, 3, index, slice(lane, lane + TOK))
            first[rows, lanes] = (upstream * slope).astype(BF16)
            if part == 0:
                second[rows, :] = (upstream * (bend * tangent[rows, :])).astype(BF16)


PAIR = (shape((WIDE, 2 * TOK), BF16), shape((WIDE, TOK), BF16), shape((2 * TOK, D), BF16))
PAIR_SCRATCH = (VMEM((WIDE, 2 * TOK), F32), VMEM((WIDE, TOK), F32), pltpu.SemaphoreType.DMA((1,)))


def early_pair_kernel(b0, b1, wt, u0, u1, u2, u3, u4, first, second, xs, pre, tangent, sems):
    pair_terms(0, (b0, b1), wt, (u0, u1, u2, u3, u4), first, second, xs, pre, tangent, sems.at[0])


def early_pair(blocks, wt, ups):
    return pl.pallas_call(
        early_pair_kernel,
        out_shape=PAIR,
        in_specs=[spec(ANY)] * 2 + [spec(VMEM)] * 6,
        out_specs=(spec(VMEM),) * 3,
        scratch_shapes=PAIR_SCRATCH,
        compiler_params=params(14),
        cost_estimate=cost(1 << 29, 8 << 20, 1 << 18),
        name="early_pair",
    )(*blocks, wt, *ups)


def late_pair_kernel(
    place, b0, b1, wt, u0, u1, u2, u3, u4, grad, early, early_xs, give, first, second, xs, pre, tangent, sems
):
    pair_terms(1, (b0, b1), wt, (u0, u1, u2, u3, u4), first, second, xs, pre, tangent, sems.at[0])
    for lanes, tile in half_tiles(1 - place[0]):
        total = grad[:, tile] + product(early[...], early_xs[:, tile]) + product(first[...], xs[:, tile])
        give[:, lanes] = total.astype(BF16)


def late_pair(place, blocks, wt, ups, grad, early, early_xs):
    return pl.pallas_call(
        late_pair_kernel,
        out_shape=(shape((WIDE, HALF), BF16),) + PAIR,
        in_specs=[spec(SMEM)] + [spec(ANY)] * 2 + [spec(VMEM)] * 9,
        out_specs=(spec(VMEM),) * 4,
        scratch_shapes=PAIR_SCRATCH,
        compiler_params=params(22),
        cost_estimate=cost(1 << 30, 12 << 20, 1 << 18),
        name="late_pair",
    )(place, *blocks, wt, *ups, grad, early, early_xs)


def last_halves_kernel(place, first0, second0, xs0, first1, second1, xs1, grad, hess, keep_grad, keep_hess, give_hess):
    core = place[0]

    def curvature_sum(tile):
        return hess[:, tile] + product(second0[...], xs0[:TOK, tile]) + product(second1[...], xs1[:TOK, tile])

    for lanes, tile in half_tiles(1 - core):
        give_hess[:, lanes] = curvature_sum(tile).astype(BF16)
    for lanes, tile in half_tiles(core):
        keep_hess[:, lanes] = curvature_sum(tile)
        keep_grad[:, lanes] = grad[:, tile] + product(first0[...], xs0[:, tile]) + product(first1[...], xs1[:, tile])


def last_halves(place, *operands):
    return pl.pallas_call(
        last_halves_kernel,
        out_shape=(shape((WIDE, HALF), F32), shape((WIDE, HALF), F32), shape((WIDE, HALF), BF16)),
        in_specs=[spec(SMEM)] + [spec(VMEM)] * 8,
        out_specs=(spec(VMEM),) * 3,
        compiler_params=params(22),
        cost_estimate=cost(1 << 30, 12 << 20),
        name="last_halves",
    )(place, *operands)


def sophia_kernel(place, grad_mine, grad_theirs, hess_mine, hess_theirs, bits, moment, curvature, s0, s1, s2, s3, *refs):
    outs, stage, sems = refs[:3], refs[3:6], refs[6]
    core = place[0]
    squares = jnp.sum((s0[...] + s1[...]) + (s2[...] + s3[...]))
    scale = jnp.minimum(1.0, lax.rsqrt(squares / (D * FF) + 1e-06))
    copies = []
    for half, grad, hess in ((core, grad_mine, hess_mine), (1 - core, grad_theirs, hess_theirs)):
        for part in range(4):
            lanes = slice(part * 256, (part + 1) * 256)
            rows = pl.ds(pl.multiple_of(half * HALF + part * 256, 256), 256)
            probe = (2 * bits[rows, :] - 1).astype(F32)
            estimate = 2.0 * scale * probe * hess[:, lanes].T
            moment_out = beta_first * moment[rows, :] + (1.0 - beta_first) * scale * grad[:, lanes].T
            curvature_out = beta_second * curvature[rows, :] + (1.0 - beta_second) * estimate
            stage[0][rows, :] = moment_out
            stage[1][rows, :] = curvature_out
            stage[2][rows, :] = jnp.clip(
                moment_out / jnp.maximum(gamma_scale * curvature_out, floor_value), -1.0, 1.0
            )
            for index in range(3):
                copy = pltpu.make_async_copy(stage[index].at[rows, :], outs[index].at[rows, :], sems.at[index])
                copy.start()
                copies.append(copy)
    wait(copies)


def sophia_step(place, sums, state, squares):
    return pl.pallas_call(
        sophia_kernel,
        out_shape=(shape((D, HID), F32),) * 3,
        in_specs=[spec(SMEM)] + [spec(VMEM)] * 11,
        out_specs=(spec(ANY),) * 3,
        scratch_shapes=[VMEM((D, HID), F32)] * 3 + [pltpu.SemaphoreType.DMA((3,))],
        compiler_params=params(14),
        cost_estimate=cost(1 << 23, 8 << 20),
        name="sophia_step",
    )(place, *sums, *state, *squares)


def four(value, axes, pairs):
    return [value] + [lax.ppermute(value, axes, pair) for pair in pairs]


YL_Z = (
    ("yl", "z"),
    [
        [(y * 8 + z, (y ^ dy) * 8 + (z ^ dz)) for y in range(2) for z in range(8)]
        for dy, dz in ((1, 0), (0, 1), (1, 1))
    ],
)
Z = ("z", [[(z, (z + by) % 8) for z in range(8)] for by in (2, 6, 4)])
X = ("x", [[(x, (x + by) % 4) for x in range(4)] for by in (1, 3, 2)])


def local(tokens, cotangent, weight, probe_bits, moment, curvature):
    place = jnp.stack([lax.axis_index(axis) for axis in ("c", "x", "z", "yl")]).astype(jnp.int32)
    core = lax.axis_index("c")

    got = {(0, 0): tokens}
    got[0, -1] = shift(tokens, "z", 1)
    got[0, 1] = shift(tokens, "z", -1)
    got[1, 0] = shift(tokens, "yl", 1)
    own, sent = pack_weights(place, weight, probe_bits)
    right, left = shift(sent, "x", 1), shift(sent, "x", -1)

    place, (got[0, -1], got[0, 1], got[1, 0]) = after(place, (got[0, -1], got[0, 1], got[1, 0]))
    got[0, -2] = shift(got[0, -1], "z", 1)
    got[0, 2] = shift(got[0, 1], "z", -1)
    got[1, -1] = shift(got[0, -1], "yl", 1)
    mine = [right, left, shift(right[:HID], "x", 1), shift(left[HID:], "x", -1)]
    turned = pack_cotangent(place, cotangent)

    (mine, turned), (got[0, -2], got[0, 2], got[1, -1]) = after((mine, turned), (got[0, -2], got[0, 2], got[1, -1]))
    got[0, -3] = shift(got[0, -2], "z", 1)
    got[0, 3] = shift(got[0, 2], "z", -1)
    got[1, -2] = shift(got[0, -2], "yl", 1)
    theirs, turned = after(shift(join(mine), "c", 1), turned)
    right, left = shift(turned[1], "x", 1), shift(turned[2], "x", -1)
    factors, wt = first_slopes(place, [got[key] for key in CHUNKS[0]], (own, *mine, theirs))

    factors, (got[0, -3], got[0, 3], got[1, -2]) = after(factors, (got[0, -3], got[0, 3], got[1, -2]))
    got[0, -4] = shift(got[0, -3], "z", 1)
    got[1, 1] = shift(got[1, 0], "z", -1)
    got[1, -3] = shift(got[0, -3], "yl", 1)
    ups = [turned[0], right, left, shift(right[HID:], "x", 1), shift(left[HID:], "x", -1)]
    factors += slopes([got[key] for key in CHUNKS[1]], wt)

    factors, (got[0, -4], got[1, 1], got[1, -3]) = after(factors, (got[0, -4], got[1, 1], got[1, -3]))
    got[1, -4] = shift(got[1, -3], "z", 1)
    got[1, 2] = shift(got[1, 1], "z", -1)
    got[1, 3] = shift(got[0, 3], "yl", 1)
    factors += slopes([got[key] for key in CHUNKS[2]], wt)
    grad, hess = products([got[key] for chunk in CHUNKS[:3] for key in chunk], ups, factors)

    (grad, hess), got[1, 3] = after((grad, hess), got[1, 3])
    early = early_pair((got[1, -3], got[1, 3]), wt, ups)
    (grad, hess, early), blocks = after((grad, hess, early), (got[1, -4], got[1, 2]))
    give_grad, *late = late_pair(place, blocks, wt, ups, grad, early[0], early[2])
    keep_grad, keep_hess, give_hess = last_halves(place, *early, *late, grad, hess)

    def over_cores(keep, give):
        keep = keep + shift(give, "c", 1).astype(F32)
        return keep[:HID], [keep[n * HID : (n + 1) * HID].astype(BF16) for n in range(1, 4)]

    def add_x(total, parts):
        for part in parts:
            total = total + part.astype(F32)
        return total.astype(BF16)

    def over_y(total):
        return total.astype(F32) + shift(total, "yh", 1).astype(F32)

    def over_x(own, sent):
        return add_x(own, [shift(part, "x", -hop) for hop, part in reversed([*zip(HOPS[1:], sent)])])

    gradient = over_y(over_x(*over_cores(keep_grad, give_grad)))
    hessian_vector = over_x(*over_cores(keep_hess, give_hess))
    gradient, hessian_vector = after(gradient, hessian_vector)
    gradients = (gradient, shift(gradient, "c", 1))
    squares = [jnp.sum((half * half).reshape(-1, 8, HALF // TOK, TOK), axis=(0, 2)) for half in gradients]
    squares, hessian_vector = after(sum(four(squares[0] + squares[1], *YL_Z)), over_y(hessian_vector))
    squares, other = after(sum(four(squares, *Z)), shift(hessian_vector, "c", 1))
    return sophia_step(
        place,
        (*gradients, hessian_vector, other),
        (probe_bits, moment, curvature),
        four(squares, *X),
    )


def solution(mesh):
    fine = Mesh(mesh.devices.reshape(tuple(SIZES.values())), AXES)
    dp, fsdp = ("yh", "c"), ("yl", "z", "x")
    return jax.shard_map(
        local,
        mesh=fine,
        in_specs=(
            P(dp + fsdp, None),
            P(dp, fsdp),
            P(None, fsdp),
            P(None, fsdp),
            P(None, fsdp),
            P(None, fsdp),
        ),
        out_specs=(P(None, fsdp), P(None, fsdp), P(None, fsdp)),
        check_vma=False,
    )
```

```python
import functools

import jax
import jax.numpy as jnp
from jax import lax
from jax.experimental import pallas as pl
from jax.experimental.pallas import tpu as pltpu
from jax.sharding import Mesh, PartitionSpec as P

D = 2048
FF = 8192
HALF = D // 2
TOK = 128
HESS = 64
HID = 128
WIDE = 4 * HID
GROUP = 4 * TOK

inv_root_two = 0.7071067811865476
inv_root_tau = 0.3989422804014327
beta_first = 0.96
beta_second = 0.99
gamma_scale = 0.5
floor_value = 0.1

SIZES = {"yl": 2, "z": 8, "x": 4, "yh": 2, "c": 2}
AXES = tuple(SIZES)
HOPS = (0, 1, -1, 2)
CHUNKS = (
    ((0, 0), (0, -1), (0, 1), (1, 0)),
    ((0, -2), (0, 2), (1, -1), (0, -3)),
    ((0, 3), (1, -2), (0, -4), (1, 1)),
    ((1, -3), (1, 3), (1, -4), (1, 2)),
)

F32, BF16 = jnp.float32, jnp.bfloat16
VMEM, SMEM, ANY = pltpu.VMEM, pltpu.SMEM, pl.ANY


def gelu_slopes(values):
    density = jnp.exp(-0.5 * values * values) * inv_root_tau
    normal_cdf = 0.5 * (1.0 + lax.erf(values * inv_root_two))
    return (normal_cdf + values * density, density * (2.0 - values * values))


def shape(dims, dtype):
    return jax.ShapeDtypeStruct(dims, dtype)


def spec(space):
    return pl.BlockSpec(memory_space=space)


def params(mib):
    return pltpu.CompilerParams(vmem_limit_bytes=mib << 20)


def cost(flops, moved, transcendentals=0):
    return pl.CostEstimate(flops=flops, bytes_accessed=moved, transcendentals=transcendentals)


def shift(value, axis, by):
    n = SIZES[axis]
    with jax.named_scope("%s%d" % (axis, by)):
        return lax.ppermute(value, axis, [(i, (i + by) % n) for i in range(n)])


def after(values, done):
    return lax.optimization_barrier((values, done))


def weights_kernel(place, weight, bits, own, mine, weight_in, bits_in, sems):
    parts = 4
    copies = []
    for part in range(parts):
        rows = pl.ds(part * (D // parts), D // parts)
        copies.append(
            [
                pltpu.make_async_copy(weight.at[rows, :], weight_in.at[rows, :], sems.at[part]),
                pltpu.make_async_copy(bits.at[rows, :], bits_in.at[rows, :], sems.at[part]),
            ]
        )
        for copy in copies[-1]:
            copy.start()
    for part in range(parts):
        for copy in copies[part]:
            copy.wait()
        rows = slice(part * (D // parts), (part + 1) * (D // parts))
        own[:HID, rows] = weight_in[rows, :].T.astype(BF16)
        own[HID:, rows] = (2 * bits_in[rows, :] - 1).astype(F32).T.astype(BF16)
    mine[...] = own[:, pl.ds(pl.multiple_of(place[0] * HALF, HALF), HALF)]


def pack_weights(place, weight, bits):
    return pl.pallas_call(
        weights_kernel,
        out_shape=(shape((2 * HID, D), BF16), shape((2 * HID, HALF), BF16)),
        in_specs=[spec(SMEM), spec(ANY), spec(ANY)],
        out_specs=(spec(VMEM), spec(VMEM)),
        scratch_shapes=[VMEM((D, HID), F32), VMEM((D, HID), jnp.int32), pltpu.SemaphoreType.DMA((4,))],
        compiler_params=params(8),
        cost_estimate=cost(1 << 20, 4 << 20),
        name="pack_weights",
    )(place, weight, bits)


def join_kernel(first, second, third, fourth, out, sems):
    copies = []
    row = 0
    for index, part in enumerate((first, second, third, fourth)):
        rows = part.shape[0]
        copies.append(pltpu.make_async_copy(part, out.at[pl.ds(row, rows), :], sems.at[index]))
        row += rows
    for copy in copies:
        copy.start()
    for copy in copies:
        copy.wait()


def join(parts):
    return pl.pallas_call(
        join_kernel,
        out_shape=shape((6 * HID, HALF), BF16),
        in_specs=[spec(ANY)] * 4,
        out_specs=spec(ANY),
        scratch_shapes=[pltpu.SemaphoreType.DMA((4,))],
        compiler_params=params(4),
        cost_estimate=cost(0, 3 << 20),
        name="join",
    )(*parts)


def cotangent_kernel(place, cotangent, own, right, left):
    x, z, yl = place[1], place[2], place[3]
    for hop in HOPS:
        for number, chunk in enumerate(CHUNKS):
            starts = []
            for other, dz in chunk:
                row = lax.rem(yl + other, 2) * 8 + lax.rem(z + (dz + 8), 8)
                starts.append((row * 4 + lax.rem(x + (hop + 4), 4)) * TOK)
            for part in range(2):
                for pair in range(2):
                    rows = [
                        cotangent[pl.ds(pl.multiple_of(start + part * HESS, HESS), HESS), :]
                        for start in starts[2 * pair : 2 * pair + 2]
                    ]
                    turned = jnp.concatenate(rows, axis=0).T
                    lane = number * GROUP + part * 2 * TOK + pair * TOK
                    lanes = slice(lane, lane + TOK)
                    if hop == 2:
                        right[HID:, lanes] = turned[: HID // 2]
                        left[HID:, lanes] = turned[HID // 2 :]
                    else:
                        out = {0: own, 1: right, -1: left}[hop]
                        out[:HID, lanes] = turned


def pack_cotangent(place, cotangent):
    sent = shape((HID + HID // 2, 4 * GROUP), BF16)
    return pl.pallas_call(
        cotangent_kernel,
        out_shape=(shape((HID, 4 * GROUP), BF16), sent, sent),
        in_specs=[spec(SMEM), spec(VMEM)],
        out_specs=(spec(VMEM),) * 3,
        compiler_params=params(10),
        cost_estimate=cost(1 << 20, 4 << 20),
        name="pack_cotangent",
    )(place, cotangent)


def product(left, right):
    return lax.dot_general(left, right, (((1,), (0,)), ((), ())), preferred_element_type=F32)


def product_nt(left, right):
    return lax.dot_general(left, right, (((1,), (1,)), ((), ())), preferred_element_type=F32)


def token_copies(blocks, xs, base, sem):
    return [
        pltpu.make_async_copy(
            block.at[pl.ds(part * HESS, HESS), :],
            xs.at[pl.ds(base + part * 2 * TOK + index * HESS, HESS), :],
            sem,
        )
        for index, block in enumerate(blocks)
        for part in range(2)
    ]


def weight_copies(core, own, mine, theirs, wt, sem):
    copies = []
    for kind in range(2):
        copies.append(pltpu.make_async_copy(own.at[pl.ds(kind * HID, HID), :], wt.at[pl.ds(kind * WIDE, HID), :], sem))
        for index in range(3):
            start_row = index * 2 * HID + kind * HID
            rows = pl.ds(kind * WIDE + (index + 1) * HID, HID)
            source = mine[index].at[pl.ds(kind * HID, HID), :] if index < 2 else mine[2 + kind]
            lanes = pl.ds(pl.multiple_of(core * HALF, HALF), HALF)
            copies.append(pltpu.make_async_copy(source, wt.at[rows, lanes], sem))
            lanes = pl.ds(pl.multiple_of((1 - core) * HALF, HALF), HALF)
            copies.append(pltpu.make_async_copy(theirs.at[pl.ds(start_row, HID), :], wt.at[rows, lanes], sem))
    return copies


def upstream_rows(ups, number, index, lanes):
    own, right, left, low, high = ups
    source, row = ((own, 0), (own, 64), (right, 0), (right, 64), (left, 0), (left, 64), (low, 0), (high, 0))[index]
    return source[row : row + 64, number * GROUP + lanes.start : number * GROUP + lanes.stop].astype(F32)


def start(copies):
    for copy in copies:
        copy.start()


def wait(copies):
    for copy in copies:
        copy.wait()


ROWS = [slice(row, row + 64) for row in range(0, WIDE, 64)]
PARTS = [slice(0, 2 * TOK), slice(2 * TOK, GROUP)]


def slopes_of(xs, wt, slope, curve, pre, tangent):
    pre[:, PARTS[0]] = product_nt(wt[:WIDE, :], xs[PARTS[0], :])
    tangent[...] = product_nt(wt[WIDE:, :], xs[PARTS[0], :])
    pre[:, PARTS[1]] = product_nt(wt[:WIDE, :], xs[PARTS[1], :])
    for rows in ROWS:
        for part, lanes in enumerate(PARTS):
            one, two = gelu_slopes(pre[rows, lanes])
            slope[rows, lanes] = one
            if part == 0:
                curve[rows, :] = two * tangent[rows, :]


def first_slopes_kernel(place, b0, b1, b2, b3, own, m0, m1, m2, m3, theirs, slope, curve, wt, xs, pre, tangent, sems):
    tokens = token_copies((b0, b1, b2, b3), xs, 0, sems.at[0])
    weights = weight_copies(place[0], own, (m0, m1, m2, m3), theirs, wt, sems.at[1])
    start(tokens)
    start(weights)
    wait(tokens)
    wait(weights)
    slopes_of(xs, wt, slope, curve, pre, tangent)


def slopes_kernel(b0, b1, b2, b3, wt, slope, curve, xs, pre, tangent, sems):
    tokens = token_copies((b0, b1, b2, b3), xs, 0, sems.at[0])
    start(tokens)
    wait(tokens)
    slopes_of(xs, wt, slope, curve, pre, tangent)


SLOPES = (shape((WIDE, GROUP), F32), shape((WIDE, 2 * TOK), F32))
SLOPES_SCRATCH = (
    VMEM((GROUP, D), BF16),
    VMEM((WIDE, GROUP), F32),
    VMEM((WIDE, 2 * TOK), F32),
    pltpu.SemaphoreType.DMA((2,)),
)


def first_slopes(place, blocks, weights):
    *factors, wt = pl.pallas_call(
        first_slopes_kernel,
        out_shape=SLOPES + (shape((2 * WIDE, D), BF16),),
        in_specs=[spec(SMEM)] + [spec(ANY)] * 10,
        out_specs=(spec(VMEM),) * 3,
        scratch_shapes=SLOPES_SCRATCH,
        compiler_params=params(14),
        cost_estimate=cost(3 << 29, 8 << 20, 1 << 19),
        name="first_slopes",
    )(place, *blocks, *weights)
    return factors, wt


def slopes(blocks, wt):
    return pl.pallas_call(
        slopes_kernel,
        out_shape=SLOPES,
        in_specs=[spec(ANY)] * 4 + [spec(VMEM)],
        out_specs=(spec(VMEM),) * 2,
        scratch_shapes=SLOPES_SCRATCH,
        compiler_params=params(14),
        cost_estimate=cost(3 << 29, 8 << 20, 1 << 19),
        name="slopes",
    )(*blocks, wt)


def products_kernel(chunks, *refs):
    blocks, ups = refs[: 4 * chunks], refs[4 * chunks : 4 * chunks + 5]
    factors = refs[4 * chunks + 5 : 6 * chunks + 5]
    grad, hess, xs, first, second, sems = refs[6 * chunks + 5 :]
    tokens = []
    for number in range(chunks):
        tokens += token_copies(blocks[4 * number : 4 * number + 4], xs, number * GROUP, sems.at[0])
    start(tokens)
    for number in range(chunks):
        slope, curve = factors[2 * number : 2 * number + 2]
        for index, rows in enumerate(ROWS):
            for part, lanes in enumerate(PARTS):
                upstream = upstream_rows(ups, number, index, lanes)
                first[rows, number * GROUP + lanes.start : number * GROUP + lanes.stop] = (
                    upstream * slope[rows, lanes]
                ).astype(BF16)
                if part == 0:
                    second[rows, number * 2 * TOK : (number + 1) * 2 * TOK] = (upstream * curve[rows, :]).astype(BF16)
    wait(tokens)
    for column in range(0, D, 256):
        lanes = slice(column, column + 256)
        grad[:, lanes] = product(first[...], xs[:, lanes])
        part = product(second[:, : 2 * TOK], xs[: 2 * TOK, lanes])
        for number in range(1, chunks):
            part += product(
                second[:, number * 2 * TOK : (number + 1) * 2 * TOK],
                xs[number * GROUP : number * GROUP + 2 * TOK, lanes],
            )
        hess[:, lanes] = part


def products(blocks, ups, factors):
    chunks = len(factors) // 2
    operands = (*blocks, *ups, *factors)
    return pl.pallas_call(
        functools.partial(products_kernel, chunks),
        out_shape=(shape((WIDE, D), F32),) * 2,
        in_specs=[spec(ANY)] * len(blocks) + [spec(VMEM)] * (len(operands) - len(blocks)),
        out_specs=(spec(VMEM),) * 2,
        scratch_shapes=[
            VMEM((chunks * GROUP, D), BF16),
            VMEM((WIDE, chunks * GROUP), BF16),
            VMEM((WIDE, chunks * 2 * TOK), BF16),
            pltpu.SemaphoreType.DMA((1,)),
        ],
        compiler_params=params(30),
        cost_estimate=cost(5 << 30, 24 << 20),
        name="products",
    )(*operands)


def half_tiles(half):
    return [
        (slice(column, column + 256), pl.ds(pl.multiple_of(half * HALF + column, 256), 256))
        for column in range(0, HALF, 256)
    ]


def pair_terms(pair, blocks, wt, ups, first, second, xs, pre, tangent, sem):
    copies = [
        pltpu.make_async_copy(
            block.at[pl.ds(part * HESS, HESS), :], xs.at[pl.ds(part * TOK + index * HESS, HESS), :], sem
        )
        for index, block in enumerate(blocks)
        for part in range(2)
    ]
    start(copies)
    wait(copies)
    pre[...] = product_nt(wt[:WIDE, :], xs[...])
    tangent[...] = product_nt(wt[WIDE:, :], xs[:TOK, :])
    for index, rows in enumerate(ROWS):
        for part in range(2):
            lanes = slice(part * TOK, (part + 1) * TOK)
            lane = part * 2 * TOK + pair * TOK
            slope, bend = gelu_slopes(pre[rows, lanes])
            upstream = upstream_rows(ups, 3, index, slice(lane, lane + TOK))
            first[rows, lanes] = (upstream * slope).astype(BF16)
            if part == 0:
                second[rows, :] = (upstream * (bend * tangent[rows, :])).astype(BF16)


PAIR = (shape((WIDE, 2 * TOK), BF16), shape((WIDE, TOK), BF16), shape((2 * TOK, D), BF16))
PAIR_SCRATCH = (VMEM((WIDE, 2 * TOK), F32), VMEM((WIDE, TOK), F32), pltpu.SemaphoreType.DMA((1,)))


def early_pair_kernel(b0, b1, wt, u0, u1, u2, u3, u4, first, second, xs, pre, tangent, sems):
    pair_terms(0, (b0, b1), wt, (u0, u1, u2, u3, u4), first, second, xs, pre, tangent, sems.at[0])


def early_pair(blocks, wt, ups):
    return pl.pallas_call(
        early_pair_kernel,
        out_shape=PAIR,
        in_specs=[spec(ANY)] * 2 + [spec(VMEM)] * 6,
        out_specs=(spec(VMEM),) * 3,
        scratch_shapes=PAIR_SCRATCH,
        compiler_params=params(14),
        cost_estimate=cost(1 << 29, 8 << 20, 1 << 18),
        name="early_pair",
    )(*blocks, wt, *ups)


def late_pair_kernel(
    place, b0, b1, wt, u0, u1, u2, u3, u4, grad, early, early_xs, give, first, second, xs, pre, tangent, sems
):
    pair_terms(1, (b0, b1), wt, (u0, u1, u2, u3, u4), first, second, xs, pre, tangent, sems.at[0])
    for lanes, tile in half_tiles(1 - place[0]):
        total = grad[:, tile] + product(early[...], early_xs[:, tile]) + product(first[...], xs[:, tile])
        give[:, lanes] = total.astype(BF16)


def late_pair(place, blocks, wt, ups, grad, early, early_xs):
    return pl.pallas_call(
        late_pair_kernel,
        out_shape=(shape((WIDE, HALF), BF16),) + PAIR,
        in_specs=[spec(SMEM)] + [spec(ANY)] * 2 + [spec(VMEM)] * 9,
        out_specs=(spec(VMEM),) * 4,
        scratch_shapes=PAIR_SCRATCH,
        compiler_params=params(22),
        cost_estimate=cost(1 << 30, 12 << 20, 1 << 18),
        name="late_pair",
    )(place, *blocks, wt, *ups, grad, early, early_xs)


def last_halves_kernel(place, first0, second0, xs0, first1, second1, xs1, grad, hess, keep_grad, keep_hess, give_hess):
    core = place[0]

    def curvature_sum(tile):
        return hess[:, tile] + product(second0[...], xs0[:TOK, tile]) + product(second1[...], xs1[:TOK, tile])

    for lanes, tile in half_tiles(1 - core):
        give_hess[:, lanes] = curvature_sum(tile).astype(BF16)
    for lanes, tile in half_tiles(core):
        keep_hess[:, lanes] = curvature_sum(tile)
        keep_grad[:, lanes] = grad[:, tile] + product(first0[...], xs0[:, tile]) + product(first1[...], xs1[:, tile])


def last_halves(place, *operands):
    return pl.pallas_call(
        last_halves_kernel,
        out_shape=(shape((WIDE, HALF), F32), shape((WIDE, HALF), F32), shape((WIDE, HALF), BF16)),
        in_specs=[spec(SMEM)] + [spec(VMEM)] * 8,
        out_specs=(spec(VMEM),) * 3,
        compiler_params=params(22),
        cost_estimate=cost(1 << 30, 12 << 20),
        name="last_halves",
    )(place, *operands)


def sophia_kernel(place, grad_mine, grad_theirs, hess_mine, hess_theirs, bits, moment, curvature, s0, s1, s2, s3, *refs):
    outs, stage, sems = refs[:3], refs[3:6], refs[6]
    core = place[0]
    squares = jnp.sum((s0[...] + s1[...]) + (s2[...] + s3[...]))
    scale = jnp.minimum(1.0, lax.rsqrt(squares / (D * FF) + 1e-06))
    copies = []
    for half, grad, hess in ((core, grad_mine, hess_mine), (1 - core, grad_theirs, hess_theirs)):
        for part in range(4):
            lanes = slice(part * 256, (part + 1) * 256)
            rows = pl.ds(pl.multiple_of(half * HALF + part * 256, 256), 256)
            probe = (2 * bits[rows, :] - 1).astype(F32)
            estimate = 2.0 * scale * probe * hess[:, lanes].T
            moment_out = beta_first * moment[rows, :] + (1.0 - beta_first) * scale * grad[:, lanes].T
            curvature_out = beta_second * curvature[rows, :] + (1.0 - beta_second) * estimate
            stage[0][rows, :] = moment_out
            stage[1][rows, :] = curvature_out
            stage[2][rows, :] = jnp.clip(
                moment_out / jnp.maximum(gamma_scale * curvature_out, floor_value), -1.0, 1.0
            )
            for index in range(3):
                copy = pltpu.make_async_copy(stage[index].at[rows, :], outs[index].at[rows, :], sems.at[index])
                copy.start()
                copies.append(copy)
    wait(copies)


def sophia_step(place, sums, state, squares):
    return pl.pallas_call(
        sophia_kernel,
        out_shape=(shape((D, HID), F32),) * 3,
        in_specs=[spec(SMEM)] + [spec(VMEM)] * 11,
        out_specs=(spec(ANY),) * 3,
        scratch_shapes=[VMEM((D, HID), F32)] * 3 + [pltpu.SemaphoreType.DMA((3,))],
        compiler_params=params(14),
        cost_estimate=cost(1 << 23, 8 << 20),
        name="sophia_step",
    )(place, *sums, *state, *squares)


def four(value, axes, pairs):
    return [value] + [lax.ppermute(value, axes, pair) for pair in pairs]


YL_Z = (
    ("yl", "z"),
    [
        [(y * 8 + z, (y ^ dy) * 8 + (z ^ dz)) for y in range(2) for z in range(8)]
        for dy, dz in ((1, 0), (0, 1), (1, 1))
    ],
)
Z = ("z", [[(z, (z + by) % 8) for z in range(8)] for by in (2, 6, 4)])
X = ("x", [[(x, (x + by) % 4) for x in range(4)] for by in (1, 3, 2)])


def local(tokens, cotangent, weight, probe_bits, moment, curvature):
    place = jnp.stack([lax.axis_index(axis) for axis in ("c", "x", "z", "yl")]).astype(jnp.int32)
    core = lax.axis_index("c")

    got = {(0, 0): tokens}
    got[0, -1] = shift(tokens, "z", 1)
    got[0, 1] = shift(tokens, "z", -1)
    got[1, 0] = shift(tokens, "yl", 1)
    own, sent = pack_weights(place, weight, probe_bits)
    right, left = shift(sent, "x", 1), shift(sent, "x", -1)

    place, (got[0, -1], got[0, 1], got[1, 0]) = after(place, (got[0, -1], got[0, 1], got[1, 0]))
    got[0, -2] = shift(got[0, -1], "z", 1)
    got[0, 2] = shift(got[0, 1], "z", -1)
    got[1, -1] = shift(got[0, -1], "yl", 1)
    mine = [right, left, shift(right[:HID], "x", 1), shift(left[HID:], "x", -1)]
    turned = pack_cotangent(place, cotangent)

    (mine, turned), (got[0, -2], got[0, 2], got[1, -1]) = after((mine, turned), (got[0, -2], got[0, 2], got[1, -1]))
    got[0, -3] = shift(got[0, -2], "z", 1)
    got[0, 3] = shift(got[0, 2], "z", -1)
    got[1, -2] = shift(got[0, -2], "yl", 1)
    theirs, turned = after(shift(join(mine), "c", 1), turned)
    right, left = shift(turned[1], "x", 1), shift(turned[2], "x", -1)
    factors, wt = first_slopes(place, [got[key] for key in CHUNKS[0]], (own, *mine, theirs))

    factors, (got[0, -3], got[0, 3], got[1, -2]) = after(factors, (got[0, -3], got[0, 3], got[1, -2]))
    got[0, -4] = shift(got[0, -3], "z", 1)
    got[1, 1] = shift(got[1, 0], "z", -1)
    got[1, -3] = shift(got[0, -3], "yl", 1)
    ups = [turned[0], right, left, shift(right[HID:], "x", 1), shift(left[HID:], "x", -1)]
    factors += slopes([got[key] for key in CHUNKS[1]], wt)

    factors, (got[0, -4], got[1, 1], got[1, -3]) = after(factors, (got[0, -4], got[1, 1], got[1, -3]))
    got[1, -4] = shift(got[1, -3], "z", 1)
    got[1, 2] = shift(got[1, 1], "z", -1)
    got[1, 3] = shift(got[0, 3], "yl", 1)
    factors += slopes([got[key] for key in CHUNKS[2]], wt)
    grad, hess = products([got[key] for chunk in CHUNKS[:3] for key in chunk], ups, factors)

    (grad, hess), got[1, 3] = after((grad, hess), got[1, 3])
    early = early_pair((got[1, -3], got[1, 3]), wt, ups)
    (grad, hess, early), blocks = after((grad, hess, early), (got[1, -4], got[1, 2]))
    give_grad, *late = late_pair(place, blocks, wt, ups, grad, early[0], early[2])
    keep_grad, keep_hess, give_hess = last_halves(place, *early, *late, grad, hess)

    def over_cores(keep, give):
        keep = keep + shift(give, "c", 1).astype(F32)
        return keep[:HID], [keep[n * HID : (n + 1) * HID].astype(BF16) for n in range(1, 4)]

    def add_x(total, parts):
        for part in parts:
            total = total + part.astype(F32)
        return total.astype(BF16)

    def over_y(total):
        return total.astype(F32) + shift(total, "yh", 1).astype(F32)

    def over_x(own, sent):
        return add_x(own, [shift(part, "x", -hop) for hop, part in reversed([*zip(HOPS[1:], sent)])])

    gradient = over_y(over_x(*over_cores(keep_grad, give_grad)))
    hessian_vector = over_x(*over_cores(keep_hess, give_hess))
    gradient, hessian_vector = after(gradient, hessian_vector)
    gradients = (gradient, shift(gradient, "c", 1))
    squares = [jnp.sum((half * half).reshape(-1, 8, HALF // TOK, TOK), axis=(0, 2)) for half in gradients]
    squares = sum(four(squares[0] + squares[1], *YL_Z))
    squares, hessian_vector = after(sum(four(squares, *Z)), over_y(hessian_vector))
    other = shift(hessian_vector, "c", 1)
    return sophia_step(
        place,
        (*gradients, hessian_vector, other),
        (probe_bits, moment, curvature),
        four(squares, *X),
    )


def solution(mesh):
    fine = Mesh(mesh.devices.reshape(tuple(SIZES.values())), AXES)
    dp, fsdp = ("yh", "c"), ("yl", "z", "x")
    return jax.shard_map(
        local,
        mesh=fine,
        in_specs=(
            P(dp + fsdp, None),
            P(dp, fsdp),
            P(None, fsdp),
            P(None, fsdp),
            P(None, fsdp),
            P(None, fsdp),
        ),
        out_specs=(P(None, fsdp), P(None, fsdp), P(None, fsdp)),
        check_vma=False,
    )
```
